32 devices in a mesh: role: 2 (over core), dp: 16 (over z, y, x).
Axes of the slice: x: 2, y: 2, z: 4, core: 2. Of those that a mesh axis runs over, the one named last changes fastest.
Arguments:
- board_now: bfloat16 [1024, 10, 10, 128], P('dp'), may hold values from -6 to 6
- traj_boards: bfloat16 [16, 16, 10, 10, 128], P('dp'), may hold values from -6 to 6
- actions: int32 [16, 16], P('dp'), may hold values from 0 to 399
- lengths: int32 [16], P('dp'), may hold values from 1 to 16, 160 in all
- behaviour: float32 [16, 16], P('dp'), may hold values from -7 to -4.5
- regular: float32 [16, 16], P('dp'), may hold values from -7 to -4.5
- rewards: float32 [16, 16], P('dp'), may hold values from -4 to 4
- torso: float32 [2304, 128], replicated, may hold values from -0.1875 to 0.1875
- policy_head: bfloat16 [128, 4], replicated, may hold values from -0.5 to 0.5
- value_head: bfloat16 [128], replicated, may hold values from -2.390625 to 2.390625
- first_moment: float32 [2304, 128], P('dp'), may hold values from -6 to 6
- second_moment: float32 [2304, 128], P('dp'), may hold values from 0.5 to 2
Outputs:
- new_weights: float32 [2304, 128], P('dp')
- move_logp: float32 [1024, 400], P('dp')
The draws below stay inside these ranges and needn't reach their ends.
Inputs may be any that keep to these rules, and one draw needn't show every extreme that they name: `lengths`: live moves of a trajectory are its first slots; some trajectory has all 16.
All inputs are finite; a program needn't handle non-finite values. No bound on the sum of `lengths` on one device may be relied on, other than what follows from the above.
Results may differ from the reference program's by a relative error of at most 0.0027.
The reference program's roundings to bfloat16 on the way (of `kernels` and `hidden`) count: a program that leaves them out, or rounds other values in their place, can miss the bound.
Values sent between devices are 32-bit elements; how exact they have to be, the bound alone decides.
A program may use at most 128 MiB of HBM per device.

```python
import math
import jax
import jax.numpy as jnp
import numpy as np
from jax import lax

CH = 128
SIDE = 10
DIRS = 4
LEN = 16
G_DEV = 64
TRAJ = 16
GAMES = 1024
NW = 2304


def plant(result, rng, least, top_value):
    dims = result.shape
    spot = [jax.random.randint(jax.random.fold_in(rng, axis), (), 0, dims[axis]) for axis in range(len(dims))]
    result = result.at[tuple(spot)].set(least)
    longest = dims.index(max(dims))
    spot[longest] = (spot[longest] + 1) % dims[longest]
    return result.at[tuple(spot)].set(top_value)


def block_scale(rng, shape, cuts, low, high):
    factor_of = 1.0
    for axis_at, blocks in cuts:
        heights = jax.random.uniform(jax.random.fold_in(jax.random.fold_in(rng, 6), axis_at), (blocks,), jnp.float32, low / len(cuts), high / len(cuts))
        factor_of = factor_of * jnp.repeat(jnp.exp(heights), shape[axis_at] // blocks).reshape((-1,) + (1,) * (len(shape) - 1 - axis_at))
    return factor_of


def length_profile(amount, total, limit, lean):
    loads = [(1 << 20) // math.isqrt(rank ** lean) + 1 for rank in range(2, amount + 1)]
    rest, given = total - limit - (amount - 1), [1] * (amount - 1)
    while rest > 0:
        candidates = [i for i in range(amount - 1) if given[i] < limit]
        mass, remaining = sum([loads[i] for i in candidates]), rest
        for i in candidates:
            more = min(limit - given[i], max(1, remaining * loads[i] // mass), rest)
            given[i] = given[i] + more
            rest = rest - more
    return np.array([limit] + given)


def uneven(own_key, amount, total, reach, slope):
    if amount == 2:
        one = jax.random.randint(own_key, (), max(1, total - reach), min(reach, total - 1) + 1)
        return jnp.stack([one, total - one])
    tallies = jnp.asarray(length_profile(amount, total, reach, slope), jnp.int32)
    pairs = (amount - 1) // 2
    giver, taker = tallies[1:1 + 2 * pairs:2], tallies[2:2 + 2 * pairs:2]
    margin = jnp.minimum(giver - 1, reach - taker)
    shifted = jax.random.randint(jax.random.fold_in(own_key, 1), (pairs,), 0, 1 << 20) % (margin + 1)
    tallies = tallies.at[1:1 + 2 * pairs:2].set(giver - shifted).at[2:2 + 2 * pairs:2].set(taker + shifted)
    return tallies[jax.random.permutation(jax.random.fold_in(own_key, 2), amount)]


def gaussian(own_key, shape, scale, most, cuts=(), kind=jnp.bfloat16):
    factor_of = block_scale(own_key, shape, cuts, -0.22, 0.18) if cuts else 1.0
    result = jax.random.normal(own_key, shape, jnp.float32) * scale * factor_of
    return jnp.minimum(jnp.maximum(result, -most), most).astype(kind)


def setup_inputs(seed: int = 0) -> dict:
    streams_of = jax.random.split(jax.random.key(seed), 13)
    return {
        "board_now": gaussian(streams_of[0], (GAMES, SIDE, SIDE, CH), 1.0, 6.0, ((0, 16),)),
        "traj_boards": gaussian(streams_of[1], (TRAJ, LEN, SIDE, SIDE, CH), 1.0, 6.0, ((0, 16),)),
        "actions": plant(jax.random.randint(streams_of[2], (TRAJ, LEN), 0, DIRS * SIDE * SIDE), jax.random.fold_in(streams_of[2], 1), 0, (DIRS * SIDE * SIDE) - 1).astype(jnp.int32),
        "lengths": uneven(streams_of[3], TRAJ, TRAJ * LEN * 5 // 8, LEN, 1).astype(jnp.int32),
        "behaviour": jnp.clip(-7.0 + 2.5 * jax.random.uniform(streams_of[4], (TRAJ, LEN), jnp.float32) ** block_scale(streams_of[4], (TRAJ, LEN), ((0, 16),), -0.2, 0.2), -7.0, -4.5),
        "regular": jnp.clip(-7.0 + 2.5 * jax.random.uniform(streams_of[5], (TRAJ, LEN), jnp.float32) ** block_scale(streams_of[5], (TRAJ, LEN), ((0, 16),), -0.2, 0.2), -7.0, -4.5),
        "rewards": gaussian(streams_of[6], (TRAJ, LEN), 1.0, 4.0, ((0, 16),), jnp.float32),
        "torso": gaussian(streams_of[7], (NW, CH), (9 * CH) ** -0.5, 0.1875, (), jnp.float32),
        "policy_head": gaussian(streams_of[8], (CH, DIRS), CH ** -0.5, 0.5),
        "value_head": gaussian(streams_of[9], (CH,), 0.4, 2.390625),
        "first_moment": gaussian(streams_of[10], (NW, CH), 1.0, 6.0, ((0, 16),), jnp.float32),
        "second_moment": jnp.clip(jnp.exp(math.log(2.0) - 1.3862944 * jax.random.uniform(streams_of[11], (NW, CH), jnp.float32) ** block_scale(streams_of[11], (NW, CH), ((0, 16),), -0.2, 0.2)), 0.5, 2.0),
    }


ETA = 0.2
LEARN_RATE = 0.03
BETA_ONE = 0.9
BETA_TWO = 0.999
ADAM_EPS = 1e-08
NORM_EPS = 1e-12

def conv_sum(boards, kernel):
    extent = boards.shape[1]
    padded = jnp.pad(boards, ((0, 0), (1, 1), (1, 1), (0, 0)))
    summed = jnp.zeros(boards.shape, jnp.float32)
    for offset in range(9):
        row_start = offset // 3
        col_start = offset % 3
        window = padded[:, row_start:row_start + extent, col_start:col_start + extent, :]
        summed = summed + jnp.dot(window, kernel[offset], preferred_element_type=jnp.float32)
    return summed

def torso_forward(boards, kernels):
    layer_inputs = []
    pre_acts = []
    hidden = boards
    for layer_index in range(kernels.shape[0]):
        pre_act = conv_sum(hidden, kernels[layer_index])
        layer_inputs.append(hidden)
        pre_acts.append(pre_act)
        hidden = (hidden.astype(jnp.float32) + jax.nn.relu(pre_act)).astype(jnp.bfloat16)
    return (hidden, layer_inputs, pre_acts)

def policy_logits(hidden, policy_head):
    per_cell = jnp.dot(hidden, policy_head, preferred_element_type=jnp.float32)
    return jnp.transpose(per_cell, (0, 3, 1, 2)).reshape(hidden.shape[0], -1)

def heads_forward(hidden, policy_head, value_head, actions):
    logits = policy_logits(hidden, policy_head)
    log_total = jnp.log(lax.optimization_barrier(jnp.sum(jnp.exp(logits), axis=1)))
    action_ids = lax.broadcasted_iota(jnp.int32, logits.shape, 1)
    picked = lax.optimization_barrier(jnp.sum(jnp.where(action_ids == actions[:, None], logits, 0.0), axis=1))
    value_cells = jnp.dot(hidden, value_head, preferred_element_type=jnp.float32)
    value_estimates = jnp.tanh(lax.optimization_barrier(jnp.mean(value_cells, axis=(1, 2))))
    return (logits, log_total, picked - log_total, value_estimates)

def vee_trace_cotangents(policy_log_probs, value_estimates, behaviour, regular, rewards, trajectory_length):
    positions = jnp.arange(policy_log_probs.shape[0], dtype=jnp.int32)
    live_mask = (positions < trajectory_length).astype(jnp.float32)
    next_live = (positions + 1 < trajectory_length).astype(jnp.float32)
    clipped_ratio = jnp.minimum(1.0, jnp.exp(policy_log_probs - behaviour))
    shaped = rewards - ETA * (policy_log_probs - regular)
    next_values = jnp.concatenate([value_estimates[1:], jnp.zeros((1,), jnp.float32)]) * next_live
    deltas = live_mask * clipped_ratio * (shaped + next_values - value_estimates)

    def backward_step(running, inputs):
        delta_now, ratio_now, live_now = inputs
        correction = live_now * (delta_now + ratio_now * running)
        return (correction, correction)
    _, corrections = lax.scan(backward_step, jnp.zeros((), jnp.float32), (deltas, clipped_ratio, live_mask), reverse=True)
    targets = value_estimates + corrections
    next_targets = jnp.concatenate([targets[1:], jnp.zeros((1,), jnp.float32)]) * next_live
    policy_gradient_term = -live_mask * clipped_ratio * (shaped + next_targets - value_estimates)
    value_gradient_term = -live_mask * (targets - value_estimates)
    return (policy_gradient_term, value_gradient_term)

def heads_backward(board_shape, policy_gradient_term, value_gradient_term, logits, log_total, value_estimates, actions, policy_head, value_head):
    probabilities = jnp.exp(logits - log_total[:, None])
    action_ids = lax.broadcasted_iota(jnp.int32, logits.shape, 1)
    onehot = (action_ids == actions[:, None]).astype(jnp.float32)
    logit_grad = policy_gradient_term[:, None] * (onehot - probabilities)
    row_count = board_shape[0]
    extent = board_shape[1]
    cell_grad = jnp.transpose(logit_grad.reshape(row_count, -1, extent, extent), (0, 2, 3, 1))
    hidden_grad = jnp.dot(cell_grad, policy_head.astype(jnp.float32).T, precision=lax.Precision.HIGHEST)
    value_cell = value_gradient_term * (1.0 - value_estimates * value_estimates) / (extent * extent)
    return hidden_grad + value_cell[:, None, None, None] * value_head.astype(jnp.float32)

def layer_backward(layer_input, pre_act, out_grad, kernel, need_input):
    extent = layer_input.shape[1]
    channels = layer_input.shape[3]
    act_grad = (out_grad * (pre_act > 0)).astype(jnp.bfloat16)
    act_rows = act_grad.reshape(-1, channels)
    padded = jnp.pad(layer_input, ((0, 0), (1, 1), (1, 1), (0, 0)))
    kernel_grads = []
    input_grad = out_grad
    for offset in range(9):
        row_start = offset // 3
        col_start = offset % 3
        window = padded[:, row_start:row_start + extent, col_start:col_start + extent, :]
        kernel_grads.append(lax.dot_general(window.reshape(-1, channels), act_rows, (((0,), (0,)), ((), ())), preferred_element_type=jnp.float32))
        if need_input:
            back_term = jnp.dot(act_grad, kernel[offset].T, preferred_element_type=jnp.float32)
            back_padded = jnp.pad(back_term, ((0, 0), (row_start, 2 - row_start), (col_start, 2 - col_start), (0, 0)))
            input_grad = input_grad + back_padded[:, 1:1 + extent, 1:1 + extent, :]
    return (jnp.stack(kernel_grads), input_grad)

def torso_backward(layer_inputs, pre_acts, hidden_grad, kernels):
    kernel_grads = [None] * kernels.shape[0]
    out_grad = hidden_grad
    for layer_index in range(kernels.shape[0] - 1, -1, -1):
        kernel_grads[layer_index], out_grad = layer_backward(layer_inputs[layer_index], pre_acts[layer_index], out_grad, kernels[layer_index], layer_index > 0)
    return jnp.stack(kernel_grads)

def trajectory_gradient(kernels, policy_head, value_head, boards, actions, behaviour, regular, rewards, trajectory_length):
    hidden, layer_inputs, pre_acts = torso_forward(boards, kernels)
    logits, log_total, policy_log_probs, value_estimates = heads_forward(hidden, policy_head, value_head, actions)
    policy_gradient_term, value_gradient_term = vee_trace_cotangents(policy_log_probs, value_estimates, behaviour, regular, rewards, trajectory_length)
    hidden_grad = heads_backward(boards.shape, policy_gradient_term, value_gradient_term, logits, log_total, value_estimates, actions, policy_head, value_head)
    return torso_backward(layer_inputs, pre_acts, hidden_grad, kernels)

def reference(board_now, traj_boards, actions, lengths, behaviour, regular, rewards, torso, policy_head, value_head, first_moment, second_moment):
    channels = torso.shape[1]
    kernels = torso.astype(jnp.bfloat16).reshape(-1, 9, channels, channels)

    def gradient_accumulator(running, inputs):
        boards_one, actions_one, behaviour_one, regular_one, single_game_rewards, length_one = inputs
        term = trajectory_gradient(kernels, policy_head, value_head, boards_one, actions_one, behaviour_one, regular_one, single_game_rewards, length_one)
        return (running + term, None)
    initial = jnp.zeros(kernels.shape, jnp.float32)
    summed_grad, _ = lax.scan(gradient_accumulator, initial, (traj_boards, actions, behaviour, regular, rewards, lengths))
    gradient = summed_grad.reshape(torso.shape)
    square_sum = jnp.sum(gradient * gradient)
    factor = jnp.minimum(1.0, jnp.sqrt(float(gradient.size)) / jnp.sqrt(square_sum + NORM_EPS))
    clipped = gradient * factor
    moment_one = BETA_ONE * first_moment + (1.0 - BETA_ONE) * clipped
    moment_two = BETA_TWO * second_moment + (1.0 - BETA_TWO) * clipped * clipped
    new_weights = torso - LEARN_RATE * moment_one / (jnp.sqrt(moment_two) + ADAM_EPS)
    new_kernels = new_weights.astype(jnp.bfloat16).reshape(-1, 9, channels, channels)
    game_blocks = board_now.reshape((GAMES // G_DEV, G_DEV) + board_now.shape[1:])

    def act_block(boards_block):
        hidden, _, _ = torso_forward(boards_block, new_kernels)
        logits = policy_logits(hidden, policy_head)
        return logits - jnp.log(lax.optimization_barrier(jnp.sum(jnp.exp(logits), axis=1, keepdims=True)))
    move_logp = lax.map(act_block, game_blocks).reshape(GAMES, -1)
    return (new_weights, move_logp)
```

```python
import functools

import jax
import jax.numpy as jnp
from jax import lax
from jax.experimental import pallas as pl
from jax.experimental.pallas import tpu as pltpu
from jax.sharding import PartitionSpec as P

ETA = 0.2
LEARN_RATE = 0.03
BETA_ONE = 0.9
BETA_TWO = 0.999
ADAM_EPS = 1e-08
NORM_EPS = 1e-12
SIDE = 10
CELLS = 100
CH = 128
TAPS = 9 * CH
F32 = jnp.float32
BF16 = jnp.bfloat16
MESH = pl.DeviceIdType.MESH


def vmem():
    return pl.BlockSpec(memory_space=pltpu.VMEM)


def fill_padded(boards, flat, padded, games):
    padded[...] = jnp.zeros(padded.shape, padded.dtype)

    def widen(step, carry):
        for part in range(10):
            at = step * 10 + part
            flat[pl.ds(pl.multiple_of(at * 16, 16), SIDE), :] = boards[at].astype(F32)
        return carry

    lax.fori_loop(0, games, widen, 0)

    def place(i, carry):
        for j in range(SIDE):
            rows = flat[pl.ds(i * 16 + j, games, stride=160), :]
            padded[i + 1, j + 1] = rows.astype(BF16)
        return carry

    lax.fori_loop(0, SIDE, place, 0)


def columns(padded, i, rows, games, flip):
    parts = []
    for p in range(3):
        for q in range(3):
            u, v = (2 - p, 2 - q) if flip else (p, q)
            window = padded[pl.ds(i + u, rows), v : v + SIDE]
            parts.append(window.reshape(rows * SIDE * games, CH))
    return jnp.concatenate(parts, axis=1)


def inner(padded, i, rows, games):
    return padded[pl.ds(i + 1, rows), 1 : 1 + SIDE].reshape(rows * SIDE * games, CH)


def lane_sum(x, games):
    shift = 64
    while shift >= games:
        x = x + pltpu.roll(x, shift, 1)
        shift //= 2
    return x


def spread_heads(head_ref, games, amount):
    rows = [jnp.broadcast_to(head_ref[d : d + 1, :], (games, CH)) for d in range(amount)]
    if games * amount < CH:
        rows.append(jnp.zeros((CH - games * amount, CH), F32))
    return jnp.concatenate(rows, axis=0).astype(BF16)


def own_lane(games):
    game = lax.broadcasted_iota(jnp.int32, (games, CH), 0)
    lane = lax.broadcasted_iota(jnp.int32, (games, CH), 1)
    return (lane % games == game).astype(F32)


def learner_kernel(
    boards,
    actions,
    lengths,
    behaviour,
    regular,
    rewards,
    torso,
    head,
    grad,
    flat,
    h0,
    h1,
    a1,
    a0,
    weights,
    turned,
    pre,
    hidden_grad,
    cells,
    small,
    heads,
    total,
):
    games, rows = 16, 2
    block = rows * SIDE * games
    role = lax.axis_index("role")
    weights[...] = torso[...].astype(BF16)
    fill_padded(boards, flat, h0, games)
    h1[...] = jnp.zeros(h1.shape, BF16)
    a1[...] = jnp.zeros(a1.shape, BF16)
    heads[...] = spread_heads(head, games, 5)
    mine = own_lane(games)

    def layer_one(step, carry):
        i = step * rows
        act = jnp.dot(columns(h0, i, rows, games, False), weights[0:TAPS], preferred_element_type=F32)
        pre[0, pl.ds(pl.multiple_of(step * block, block), block)] = act
        h = (inner(h0, i, rows, games).astype(F32) + jnp.maximum(act, 0.0)).astype(BF16)
        h1[pl.ds(i + 1, rows), 1 : 1 + SIDE] = h.reshape(rows, SIDE, games, CH)
        return carry

    lax.fori_loop(0, SIDE // rows, layer_one, 0)

    def layer_two(step, carry):
        i = step * rows
        act = jnp.dot(
            columns(h1, i, rows, games, False), weights[TAPS : 2 * TAPS], preferred_element_type=F32
        )
        pre[1, pl.ds(pl.multiple_of(step * block, block), block)] = act
        h = (inner(h1, i, rows, games).astype(F32) + jnp.maximum(act, 0.0)).astype(BF16)
        out = lax.dot_general(h, heads[...], (((1,), (1,)), ((), ())), preferred_element_type=F32)
        picked = jnp.sum(out.reshape(rows * SIDE, games, CH) * mine[None], axis=1)
        cells[pl.ds(i, rows)] = picked.reshape(rows, SIDE, CH)
        return carry

    lax.fori_loop(0, SIDE // rows, layer_two, 0)

    small[...] = jnp.zeros(small.shape, F32)
    small[0:1, 0:games] = actions[...].astype(F32)
    small[1:2, 0:games] = behaviour[...]
    small[2:3, 0:games] = regular[...]
    small[3:4, 0:games] = rewards[...]
    given = lane_sum(small[...], games)
    action = given[0:1].astype(jnp.int32)
    behave, regul, reward = given[1:2], given[2:3], given[3:4]

    lane = lax.broadcasted_iota(jnp.int32, (1, CH), 1)
    slot = lane % games
    policy_lane = lane < 4 * games
    logits = cells[...]
    cell_id = lax.broadcasted_iota(jnp.int32, logits.shape, 0) * SIDE + lax.broadcasted_iota(
        jnp.int32, logits.shape, 1
    )
    lane_full = lax.broadcasted_iota(jnp.int32, logits.shape, 2)
    taken = (lane_full // games) * CELLS + cell_id == action.reshape(1, 1, CH)
    policy_full = lane_full < 4 * games
    taken = jnp.where(policy_full, jnp.where(taken, 1.0, 0.0), 0.0)
    logits = jnp.where(policy_full, logits, 0.0)

    def over_cells(x):
        return jnp.sum(jnp.sum(x, axis=0), axis=0, keepdims=True)

    exps = jnp.where(policy_full, jnp.exp(logits), 0.0)
    log_total = jnp.log(lane_sum(over_cells(exps), games))
    logp = lane_sum(over_cells(taken * logits), games) - log_total
    value_lane = jnp.where((lane >= 4 * games) & (lane < 5 * games), 1.0, 0.0)
    values = jnp.tanh(lane_sum(over_cells(cells[...]) * value_lane, games) / CELLS)

    def ahead(x, by):
        return jnp.where(slot + by < games, pltpu.roll(x, CH - by, 1), 0.0)

    length = lengths[0]
    live = jnp.where(slot < length, 1.0, 0.0)
    next_live = jnp.where(slot + 1 < length, 1.0, 0.0)
    ratio = jnp.minimum(1.0, jnp.exp(logp - behave))
    shaped = reward - ETA * (logp - regul)
    delta = live * ratio * (shaped + ahead(values, 1) * next_live - values)
    correction, slope = live * delta, live * ratio
    by = 1
    while by < games:
        correction = correction + slope * ahead(correction, by)
        slope = slope * ahead(slope, by)
        by *= 2
    targets = values + correction
    policy_term = -live * ratio * (shaped + ahead(targets, 1) * next_live - values)
    value_term = -live * (targets - values)
    value_cell = value_term * (1.0 - values * values) / CELLS * value_lane

    probs = jnp.exp(logits - log_total.reshape(1, 1, CH))
    cells[...] = jnp.where(
        policy_full,
        policy_term.reshape(1, 1, CH) * (taken - probs),
        jnp.broadcast_to(value_cell.reshape(1, 1, CH), logits.shape),
    )

    def top(step, carry):
        i = step * rows
        at = pl.ds(pl.multiple_of(step * block, block), block)
        g = cells[pl.ds(i, rows)].reshape(rows * SIDE, 1, CH) * mine[None]
        g = g.reshape(block, CH)
        high = g.astype(BF16)
        low = (g - high.astype(F32)).astype(BF16)
        out = jnp.dot(high, heads[...], preferred_element_type=F32)
        out = out + jnp.dot(low, heads[...], preferred_element_type=F32)
        hidden_grad[at] = out
        act = jnp.where(pre[1, at] > 0, out, 0.0).astype(BF16)
        a1[pl.ds(i + 1, rows), 1 : 1 + SIDE] = act.reshape(rows, SIDE, games, CH)
        return carry

    lax.fori_loop(0, SIDE // rows, top, 0)

    def weight_grad(h, a):
        total[...] = jnp.zeros(total.shape, F32)

        def add(step, carry):
            i = step * rows
            total[...] += lax.dot_general(
                inner(h, i, rows, games),
                columns(a, i, rows, games, True),
                (((0,), (0,)), ((), ())),
                preferred_element_type=F32,
            )
            return carry

        lax.fori_loop(0, SIDE // rows, add, 0)
        for offset in range(9):
            grad[offset * CH : (offset + 1) * CH, :] = total[:, offset * CH : (offset + 1) * CH]

    @pl.when(role == 1)
    def _():
        weight_grad(h1, a1)

    @pl.when(role == 0)
    def _():
        a0[...] = jnp.zeros(a0.shape, BF16)
        for offset in range(9):
            at = TAPS + offset * CH
            turned[offset * CH : (offset + 1) * CH, :] = weights[at : at + CH, :].astype(F32).T.astype(BF16)

        def back(step, carry):
            i = step * rows
            at = pl.ds(pl.multiple_of(step * block, block), block)
            out = hidden_grad[at] + jnp.dot(
                columns(a1, i, rows, games, True), turned[...], preferred_element_type=F32
            )
            act = jnp.where(pre[0, at] > 0, out, 0.0).astype(BF16)
            a0[pl.ds(i + 1, rows), 1 : 1 + SIDE] = act.reshape(rows, SIDE, games, CH)
            return carry

        lax.fori_loop(0, SIDE // rows, back, 0)
        weight_grad(h0, a0)


def learner(boards, actions, lengths, behaviour, regular, rewards, torso, head):
    padded = (SIDE + 2, SIDE + 2, 16, CH)
    in_specs = [vmem() for _ in range(8)]
    in_specs[2] = pl.BlockSpec(memory_space=pltpu.SMEM)
    return pl.pallas_call(
        learner_kernel,
        out_shape=jax.ShapeDtypeStruct((TAPS, CH), F32),
        in_specs=in_specs,
        out_specs=vmem(),
        scratch_shapes=[
            pltpu.VMEM((16 * 160, CH), F32),
            pltpu.VMEM(padded, BF16),
            pltpu.VMEM(padded, BF16),
            pltpu.VMEM(padded, BF16),
            pltpu.VMEM(padded, BF16),
            pltpu.VMEM((2 * TAPS, CH), BF16),
            pltpu.VMEM((TAPS, CH), BF16),
            pltpu.VMEM((2, 1600, CH), F32),
            pltpu.VMEM((1600, CH), F32),
            pltpu.VMEM((SIDE, SIDE, CH), F32),
            pltpu.VMEM((8, CH), F32),
            pltpu.VMEM((CH, CH), BF16),
            pltpu.VMEM((CH, TAPS), F32),
        ],
        compiler_params=pltpu.CompilerParams(vmem_limit_bytes=48 << 20),
    )(boards, actions, lengths, behaviour, regular, rewards, torso, head)


def update_kernel(
    grad,
    torso,
    moment_one,
    moment_two,
    out,
    plane,
    quarter,
    line,
    norms,
    s1,
    r1,
    s2,
    r2,
    sn,
    rn,
    sz,
    rz,
    sp,
    rp,
    ss,
    rs,
):
    share = moment_one.shape[0]
    role = lax.axis_index("role")
    dp = lax.axis_index("dp")
    z, spot = dp // 4, dp % 4
    owner = z // 2 == role

    def send(src, dst, send_sem, recv_sem, to_role, to_dp):
        copy = pltpu.make_async_remote_copy(
            src_ref=src,
            dst_ref=dst,
            send_sem=send_sem,
            recv_sem=recv_sem,
            device_id=(to_role, to_dp),
            device_id_type=MESH,
        )
        return copy

    barrier = pltpu.get_barrier_semaphore()

    def greet(to_role, to_dp):
        pl.semaphore_signal(barrier, inc=1, device_id=(to_role, to_dp), device_id_type=MESH)

    @pl.when(owner)
    def _():
        for k in range(1, 16):
            other = (dp + k) % 16
            greet(other // 8, other)
        for o in range(2):
            greet(role, (2 - 2 * role + o) * 4 + spot)
        greet(1 - role, dp)
        pl.semaphore_wait(barrier, 18)

    @pl.when(jnp.logical_not(owner))
    def _():
        for k in range(1, 4):
            greet(role, z * 4 + (spot + k) % 4)
            greet(role, ((z + k) % 4) * 4 + spot)
        greet(1 - role, dp)
        pl.semaphore_wait(barrier, 7)

    def rows(index):
        return pl.ds(pl.multiple_of(index * share, 8), share)

    def to_plane(o, k):
        p = (spot + k) % 4
        return send(
            grad.at[rows(4 * o + p)],
            plane.at[o, spot],
            s1.at[o, k - 1],
            r1.at[o, spot],
            role,
            z * 4 + p,
        )

    def from_plane(o, k):
        p = (spot + k) % 4
        return send(
            grad.at[rows(4 * o + p)], plane.at[o, p], s1.at[o, k - 1], r1.at[o, p], role, z * 4 + p
        )

    for o in range(2):
        for k in range(1, 4):
            to_plane(o, k).start()

    def to_owner(o):
        return send(
            quarter.at[o], line.at[z], s2.at[o], r2.at[z], role, (2 * role + o) * 4 + spot
        )

    for o in range(2):
        summed = grad[rows(4 * o + spot)]
        for k in range(1, 4):
            from_plane(o, k).wait_recv()
            summed = summed + plane[o, (spot + k) % 4]
        quarter[o] = summed

        @pl.when(z != 2 * role + o)
        def _():
            to_owner(o).start()

    def to_norm(k):
        other = (dp + k) % 16
        return send(norms.at[dp], norms.at[dp], sn.at[k - 1], rn.at[dp], other // 8, other)

    def from_norm(k):
        other = (dp + k) % 16
        return send(norms.at[other], norms.at[other], sn.at[k - 1], rn.at[other], other // 8, other)

    def share_ref(to, index):
        return out.at[rows(index)]

    def down_line(k):
        return send(
            out.at[rows(dp)],
            out.at[rows(dp)],
            sz.at[k - 1],
            rz.at[z % 2],
            role,
            ((z + k) % 4) * 4 + spot,
        )

    @pl.when(owner)
    def _():
        summed = quarter[z % 2]
        for k in range(1, 4):
            other = (z + k) % 4
            send(
                quarter.at[0], line.at[other], s2.at[0], r2.at[other], role, other * 4 + spot
            ).wait_recv()
            summed = summed + line[other]
        norms[dp] = jnp.sum((summed * summed).reshape(share // 8, 8, CH), axis=0)
        for k in range(1, 16):
            to_norm(k).start()
        for k in range(1, 16):
            from_norm(k).wait_recv()
        square_sum = jnp.sum(jnp.sum(norms[...], axis=0), axis=0, keepdims=True)
        square_sum = jnp.sum(square_sum, axis=1, keepdims=True)
        size = float(torso.shape[0] * torso.shape[1])
        factor = jnp.minimum(1.0, jnp.sqrt(jnp.full((1, 1), size, F32)) / jnp.sqrt(square_sum + NORM_EPS))
        clipped = summed * factor
        one = BETA_ONE * moment_one[...] + (1.0 - BETA_ONE) * clipped
        two = BETA_TWO * moment_two[...] + (1.0 - BETA_TWO) * clipped * clipped
        out[rows(dp)] = torso[rows(dp)] - LEARN_RATE * one / (jnp.sqrt(two) + ADAM_EPS)
        for k in range(1, 4):
            down_line(k).start()

    def to_peer(o, k):
        p = (spot + k) % 4
        at = out.at[rows((2 * role + o) * 4 + spot)]
        return send(at, at, sp.at[o, k - 1], rp.at[o, spot], role, z * 4 + p)

    def to_sibling(o, k):
        p = (spot + k) % 4
        at = out.at[rows((2 * role + o) * 4 + p)]
        return send(at, at, ss.at[o, k], rs.at[o, p], 1 - role, dp)

    for o in range(2):
        at = out.at[rows((2 * role + o) * 4 + spot)]

        @pl.when(z != 2 * role + o)
        def _():
            send(at, at, sz.at[0], rz.at[o], role, (2 * role + o) * 4 + spot).wait_recv()

        for k in range(1, 4):
            to_peer(o, k).start()
        to_sibling(o, 0).start()
    for o in range(2):
        for k in range(1, 4):
            p = (spot + k) % 4
            at = out.at[rows((2 * role + o) * 4 + p)]
            send(at, at, sp.at[o, k - 1], rp.at[o, p], role, z * 4 + p).wait_recv()
            to_sibling(o, k).start()
    for o in range(2):
        for p in range(4):
            at = out.at[rows((2 - 2 * role + o) * 4 + p)]
            send(at, at, ss.at[o, p], rs.at[o, p], 1 - role, dp).wait_recv()
    for o in range(2):
        for k in range(1, 4):
            to_plane(o, k).wait_send()
            to_peer(o, k).wait_send()
        for k in range(4):
            to_sibling(o, k).wait_send()

        @pl.when(z != 2 * role + o)
        def _():
            to_owner(o).wait_send()

    @pl.when(owner)
    def _():
        for k in range(1, 16):
            to_norm(k).wait_send()
        for k in range(1, 4):
            down_line(k).wait_send()


def update_any(grad, torso, moment_one, moment_two):
    share = moment_one.shape[0]
    summed = lax.all_gather(lax.psum(grad, "dp"), "role", axis=0, tiled=True)
    start = lax.axis_index("dp") * share
    square_sum = jnp.sum(summed * summed)
    factor = jnp.minimum(1.0, jnp.sqrt(float(summed.size)) / jnp.sqrt(square_sum + NORM_EPS))
    clipped = lax.dynamic_slice_in_dim(summed, start, share, 0) * factor
    one = BETA_ONE * moment_one + (1.0 - BETA_ONE) * clipped
    two = BETA_TWO * moment_two + (1.0 - BETA_TWO) * clipped * clipped
    old = lax.dynamic_slice_in_dim(torso, start, share, 0)
    new = old - LEARN_RATE * one / (jnp.sqrt(two) + ADAM_EPS)
    return lax.all_gather(new, "dp", axis=0, tiled=True)


def update(grad, torso, moment_one, moment_two):
    share = moment_one.shape[0]
    if lax.axis_size("dp") != 16 or lax.axis_size("role") != 2:
        return update_any(grad, torso, moment_one, moment_two)
    dma = pltpu.SemaphoreType.DMA
    return pl.pallas_call(
        update_kernel,
        out_shape=jax.ShapeDtypeStruct(torso.shape, F32),
        in_specs=[vmem() for _ in range(4)],
        out_specs=vmem(),
        scratch_shapes=[
            pltpu.VMEM((2, 4, share, CH), F32),
            pltpu.VMEM((2, share, CH), F32),
            pltpu.VMEM((4, share, CH), F32),
            pltpu.VMEM((16, 8, CH), F32),
            dma((2, 3)),
            dma((2, 4)),
            dma((2,)),
            dma((4,)),
            dma((15,)),
            dma((16,)),
            dma((3,)),
            dma((2,)),
            dma((2, 3)),
            dma((2, 4)),
            dma((2, 4)),
            dma((2, 4)),
        ],
        compiler_params=pltpu.CompilerParams(
            collective_id=0, has_side_effects=True, vmem_limit_bytes=32 << 20
        ),
    )(grad, torso, moment_one, moment_two)


def actor_kernel(games, boards, torso, head, out, raw, flat, h0, h1, weights, cells, heads, sem):
    rows = 1
    block = rows * SIDE * games
    role = lax.axis_index("role")
    start = pl.multiple_of(role * games * SIDE, 8)
    copy = pltpu.make_async_copy(boards.at[pl.ds(start, games * SIDE)], raw, sem)
    copy.start()
    weights[...] = torso[...].astype(BF16)
    h1[...] = jnp.zeros(h1.shape, BF16)
    heads[...] = spread_heads(head, games, 4)
    cells[...] = jnp.zeros(cells.shape, F32)
    copy.wait()
    fill_padded(raw, flat, h0, games)
    mine = own_lane(games)

    def layer_one(step, carry):
        i = step * rows
        act = jnp.dot(columns(h0, i, rows, games, False), weights[0:TAPS], preferred_element_type=F32)
        h = (inner(h0, i, rows, games).astype(F32) + jnp.maximum(act, 0.0)).astype(BF16)
        h1[pl.ds(i + 1, rows), 1 : 1 + SIDE] = h.reshape(rows, SIDE, games, CH)
        return carry

    lax.fori_loop(0, SIDE // rows, layer_one, 0)

    def layer_two(step, carry):
        i = step * rows
        act = jnp.dot(
            columns(h1, i, rows, games, False), weights[TAPS : 2 * TAPS], preferred_element_type=F32
        )
        h = (inner(h1, i, rows, games).astype(F32) + jnp.maximum(act, 0.0)).astype(BF16)
        res = lax.dot_general(h, heads[...], (((1,), (1,)), ((), ())), preferred_element_type=F32)
        picked = jnp.sum(res.reshape(rows * SIDE, games, CH) * mine[None], axis=1)
        cells[pl.ds(step * SIDE, SIDE), :] = picked
        return carry

    lax.fori_loop(0, SIDE // rows, layer_two, 0)
    logits = cells[...]
    cell_id = lax.broadcasted_iota(jnp.int32, logits.shape, 0)
    exps = jnp.where(cell_id < CELLS, jnp.exp(logits), 0.0)
    log_total = jnp.log(lane_sum(jnp.sum(exps, axis=0, keepdims=True), games))
    turned = (logits - log_total).T
    for d in range(4):
        out[:, d * CELLS : (d + 1) * CELLS] = turned[d * games : (d + 1) * games, 0:CELLS]


def actor(boards, torso, head, games):
    padded = (SIDE + 2, SIDE + 2, games, CH)
    return pl.pallas_call(
        functools.partial(actor_kernel, games),
        out_shape=jax.ShapeDtypeStruct((games, 4 * CELLS), F32),
        in_specs=[pl.BlockSpec(memory_space=pl.ANY), vmem(), vmem()],
        out_specs=vmem(),
        scratch_shapes=[
            pltpu.VMEM((games * SIDE, SIDE, CH), BF16),
            pltpu.VMEM((games * 160, CH), F32),
            pltpu.VMEM(padded, BF16),
            pltpu.VMEM(padded, BF16),
            pltpu.VMEM((2 * TAPS, CH), BF16),
            pltpu.VMEM((CH, CH), F32),
            pltpu.VMEM((CH, CH), BF16),
            pltpu.SemaphoreType.DMA,
        ],
        compiler_params=pltpu.CompilerParams(vmem_limit_bytes=48 << 20),
    )(boards, torso, head)


def join_kernel(part, out, send_sem, recv_sem):
    games = part.shape[0]
    role = lax.axis_index("role")
    dp = lax.axis_index("dp")
    barrier = pltpu.get_barrier_semaphore()
    pl.semaphore_signal(barrier, inc=1, device_id=(1 - role, dp), device_id_type=MESH)
    pl.semaphore_wait(barrier, 1)
    mine = pl.ds(pl.multiple_of(role * games, 8), games)
    copy = pltpu.make_async_remote_copy(
        src_ref=part,
        dst_ref=out.at[mine],
        send_sem=send_sem,
        recv_sem=recv_sem,
        device_id=(1 - role, dp),
        device_id_type=MESH,
    )
    copy.start()
    out[mine] = part[...]
    copy.wait()


def join(part):
    return pl.pallas_call(
        join_kernel,
        out_shape=jax.ShapeDtypeStruct((2 * part.shape[0], part.shape[1]), F32),
        in_specs=[vmem()],
        out_specs=vmem(),
        scratch_shapes=[pltpu.SemaphoreType.DMA, pltpu.SemaphoreType.DMA],
        compiler_params=pltpu.CompilerParams(collective_id=1, has_side_effects=True),
    )(part)


def body(
    board_now,
    traj_boards,
    actions,
    lengths,
    behaviour,
    regular,
    rewards,
    torso,
    policy_head,
    value_head,
    first_moment,
    second_moment,
):
    dp_index = lax.axis_index("dp")
    head = jnp.concatenate(
        [policy_head.T, value_head[None, :], jnp.zeros((3, CH), BF16)], axis=0
    ).astype(F32)
    boards = traj_boards.reshape(-1, SIDE, CH)
    grad = learner(boards, actions, lengths, behaviour, regular, rewards, torso, head)
    weights = update(grad, torso, first_moment, second_moment)
    share_rows = first_moment.shape[0]
    new_share = lax.dynamic_slice_in_dim(weights, dp_index * share_rows, share_rows, 0)
    games = board_now.shape[0] // 2
    part = actor(board_now.reshape(-1, SIDE, CH), weights, head, games)
    return (new_share, join(part))


def solution(mesh):
    return jax.shard_map(
        body,
        mesh=mesh,
        in_specs=(
            P("dp", None, None, None),
            P("dp", None, None, None, None),
            P("dp", None),
            P("dp"),
            P("dp", None),
            P("dp", None),
            P("dp", None),
            P(),
            P(),
            P(),
            P("dp", None),
            P("dp", None),
        ),
        out_specs=(P("dp", None), P("dp", None)),
        check_vma=False,
    )
```

```python
import functools

import jax
import jax.numpy as jnp
from jax import lax
from jax.experimental import pallas as pl
from jax.experimental.pallas import tpu as pltpu
from jax.sharding import PartitionSpec as P

ETA = 0.2
LEARN_RATE = 0.03
BETA_ONE = 0.9
BETA_TWO = 0.999
ADAM_EPS = 1e-08
NORM_EPS = 1e-12
SIDE = 10
CELLS = 100
CH = 128
TAPS = 9 * CH
ROWS = 5
F32 = jnp.float32
BF16 = jnp.bfloat16
MESH = pl.DeviceIdType.MESH


def vmem():
    return pl.BlockSpec(memory_space=pltpu.VMEM)


def columns(padded, i, games, flip, first=0, last=9):
    parts = []
    for offset in range(first, last):
        p, q = offset // 3, offset % 3
        u, v = (2 - p, 2 - q) if flip else (p, q)
        window = padded[pl.ds(i + u, ROWS), v : v + SIDE]
        parts.append(window.reshape(ROWS * SIDE * games, CH))
    return jnp.concatenate(parts, axis=1)


def inner(padded, i, games):
    return padded[pl.ds(i + 1, ROWS), 1 : 1 + SIDE].reshape(ROWS * SIDE * games, CH)


def set_inner(padded, i, games, value):
    padded[pl.ds(i + 1, ROWS), 1 : 1 + SIDE] = value.reshape(ROWS, SIDE, games, CH)


def clear_rim(padded):
    zero = jnp.zeros((1, SIDE + 2) + padded.shape[2:], padded.dtype)
    side = jnp.zeros((SIDE, 1) + padded.shape[2:], padded.dtype)
    padded[0:1] = zero
    padded[SIDE + 1 : SIDE + 2] = zero
    padded[1 : SIDE + 1, 0:1] = side
    padded[1 : SIDE + 1, SIDE + 1 : SIDE + 2] = side


def center(padded):
    return padded.at[pl.ds(1, SIDE), pl.ds(1, SIDE)]


def steps(f):
    def one(step, carry):
        f(step, step * ROWS)
        return carry

    lax.fori_loop(0, SIDE // ROWS, one, 0)


def lane_sum(x, games):
    shift = 64
    while shift >= games:
        x = x + pltpu.roll(x, shift, 1)
        shift //= 2
    return x


def spread_heads(given, games, amount):
    rows = [jnp.broadcast_to(given[d : d + 1, :], (games, CH)) for d in range(amount)]
    if games * amount < CH:
        rows.append(jnp.zeros((CH - games * amount, CH), F32))
    return jnp.concatenate(rows, axis=0).astype(BF16)


def own_lane(games):
    game = lax.broadcasted_iota(jnp.int32, (games, CH), 0)
    lane = lax.broadcasted_iota(jnp.int32, (games, CH), 1)
    return (lane % games == game).astype(F32)


def head_cells(h, heads, mine, games):
    out = lax.dot_general(h, heads[...], (((1,), (1,)), ((), ())), preferred_element_type=F32)
    return jnp.sum(out.reshape(ROWS * SIDE, games, CH) * mine[None], axis=1)


def advance(source, i, games, layer_weights):
    act = jnp.dot(columns(source, i, games, False), layer_weights, preferred_element_type=F32)
    return act, (inner(source, i, games).astype(F32) + jnp.maximum(act, 0.0)).astype(BF16)


def trace_terms(logits_ref, given, games):
    spread = lane_sum(given[8:16], games)
    action = spread[0:1].astype(jnp.int32)
    behave, regul, reward = spread[1:2], spread[2:3], spread[3:4]
    lane = lax.broadcasted_iota(jnp.int32, (1, CH), 1)
    slot = lane % games
    every = logits_ref[...]
    cell_id = lax.broadcasted_iota(jnp.int32, every.shape, 0) * SIDE + lax.broadcasted_iota(
        jnp.int32, every.shape, 1
    )
    lane_full = lax.broadcasted_iota(jnp.int32, every.shape, 2)
    policy_full = lane_full < 4 * games
    taken = (lane_full // games) * CELLS + cell_id == action.reshape(1, 1, CH)
    taken = jnp.where(policy_full, jnp.where(taken, 1.0, 0.0), 0.0)
    logits = jnp.where(policy_full, every, 0.0)

    def over_cells(x):
        return jnp.sum(jnp.sum(x, axis=0), axis=0, keepdims=True)

    exps = jnp.where(policy_full, jnp.exp(logits), 0.0)
    log_total = jnp.log(lane_sum(over_cells(exps), games))
    logp = lane_sum(over_cells(taken * logits), games) - log_total
    value_lane = jnp.where((lane >= 4 * games) & (lane < 5 * games), 1.0, 0.0)
    values = jnp.tanh(lane_sum(over_cells(every) * value_lane, games) / CELLS)

    def ahead(x, by):
        return jnp.where(slot + by < games, pltpu.roll(x, CH - by, 1), 0.0)

    length = given[5:6]
    place = slot.astype(F32)
    live = jnp.where(place < length, 1.0, 0.0)
    next_live = jnp.where(place + 1.0 < length, 1.0, 0.0)
    ratio = jnp.minimum(1.0, jnp.exp(logp - behave))
    shaped = reward - ETA * (logp - regul)
    delta = live * ratio * (shaped + ahead(values, 1) * next_live - values)
    correction, slope = live * delta, live * ratio
    by = 1
    while by < games:
        correction = correction + slope * ahead(correction, by)
        slope = slope * ahead(slope, by)
        by *= 2
    targets = values + correction
    policy_term = -live * ratio * (shaped + ahead(targets, 1) * next_live - values)
    value_term = -live * (targets - values)
    value_cell = value_term * (1.0 - values * values) / CELLS * value_lane
    probs = jnp.exp(logits - log_total.reshape(1, 1, CH))
    logits_ref[...] = jnp.where(
        policy_full,
        policy_term.reshape(1, 1, CH) * (taken - probs),
        jnp.broadcast_to(value_cell.reshape(1, 1, CH), logits.shape),
    )


def learner_part(given, grad, weights, scratch, after_half):
    hs, acts, turned, pre, hidden_grad, cells, heads, total = scratch
    games = 16
    block = ROWS * SIDE * games
    role = lax.axis_index("role")
    h0, h1, a0, a1 = hs.at[0], hs.at[1], acts.at[0], acts.at[1]
    heads[...] = spread_heads(given, games, 5)
    mine = own_lane(games)

    def layer_one(step, i):
        act, h = advance(h0, i, games, weights[0:TAPS])
        pre[0, pl.ds(pl.multiple_of(step * block, block), block)] = act
        set_inner(h1, i, games, h)

    steps(layer_one)

    def layer_two(step, i):
        act, h = advance(h1, i, games, weights[TAPS : 2 * TAPS])
        pre[1, pl.ds(pl.multiple_of(step * block, block), block)] = act
        cells[pl.ds(i, ROWS)] = head_cells(h, heads, mine, games).reshape(ROWS, SIDE, CH)

    steps(layer_two)
    trace_terms(cells, given, games)

    def top(step, i):
        at = pl.ds(pl.multiple_of(step * block, block), block)
        g = cells[pl.ds(i, ROWS)].reshape(ROWS * SIDE, 1, CH) * mine[None]
        g = g.reshape(block, CH)
        high = g.astype(BF16)
        low = (g - high.astype(F32)).astype(BF16)
        out = jnp.dot(high, heads[...], preferred_element_type=F32)
        out = out + jnp.dot(low, heads[...], preferred_element_type=F32)
        hidden_grad[at] = out
        set_inner(a1, i, games, jnp.where(pre[1, at] > 0, out, 0.0).astype(BF16))

    steps(top)

    @pl.when(role == 0)
    def _():
        for offset in range(9):
            at = TAPS + offset * CH
            turned[offset * CH : (offset + 1) * CH, :] = (
                weights[at : at + CH, :].astype(F32).T.astype(BF16)
            )

        def back(step, i):
            at = pl.ds(pl.multiple_of(step * block, block), block)
            out = hidden_grad[at] + jnp.dot(
                columns(a1, i, games, True), turned[...], preferred_element_type=F32
            )
            set_inner(a0, i, games, jnp.where(pre[0, at] > 0, out, 0.0).astype(BF16))

        steps(back)

    h, a = hs.at[role], acts.at[role]
    for half, (first, last) in enumerate(((0, 5), (5, 9))):
        lanes = slice(first * CH, last * CH)

        def product(i):
            return lax.dot_general(
                inner(h, i, games),
                columns(a, i, games, True, first, last),
                (((0,), (0,)), ((), ())),
                preferred_element_type=F32,
            )

        summed = product(0)
        for step in range(1, SIDE // ROWS):
            summed = summed + product(step * ROWS)
        for offset in range(first, last):
            at = (offset - first) * CH
            grad[offset * CH : (offset + 1) * CH, :] = summed[:, at : at + CH]
        after_half(half)


def learner_scratch():
    padded = (2, SIDE + 2, SIDE + 2, 16, CH)
    return [
        pltpu.VMEM(padded, BF16),
        pltpu.VMEM(padded, BF16),
        pltpu.VMEM((TAPS, CH), BF16),
        pltpu.VMEM((2, 1600, CH), F32),
        pltpu.VMEM((1600, CH), F32),
        pltpu.VMEM((SIDE, SIDE, CH), F32),
        pltpu.VMEM((CH, CH), BF16),
        pltpu.VMEM((8, CH), F32),
    ]


def actor_part(given, weights, scratch, games, out, start, ready):
    h0, h1, cells, heads = scratch
    heads[...] = spread_heads(given, games, 4)
    cells[...] = jnp.zeros(cells.shape, F32)
    mine = own_lane(games)
    ready(0)

    def layer_one(step, i):
        _, h = advance(h0, i, games, weights[0:TAPS])
        set_inner(h1, i, games, h)

    steps(layer_one)
    ready(1)

    def layer_two(step, i):
        _, h = advance(h1, i, games, weights[TAPS : 2 * TAPS])
        found = head_cells(h, heads, mine, games).reshape(ROWS, SIDE, CH)
        for part in range(ROWS):
            cells[pl.ds((i + part) * SIDE, SIDE), :] = found[part]

    steps(layer_two)
    logits = cells[...]
    cell_id = lax.broadcasted_iota(jnp.int32, logits.shape, 0)
    exps = jnp.where(cell_id < CELLS, jnp.exp(logits), 0.0)
    log_total = jnp.log(lane_sum(jnp.sum(exps, axis=0, keepdims=True), games))
    turned = (logits - log_total).T
    for d in range(4):
        out[pl.ds(start, games), d * CELLS : (d + 1) * CELLS] = turned[
            d * games : (d + 1) * games, 0:CELLS
        ]


def actor_scratch(games):
    padded = (SIDE + 2, SIDE + 2, games, CH)
    return [
        pltpu.VMEM(padded, BF16),
        pltpu.VMEM(padded, BF16),
        pltpu.VMEM((CH, CH), F32),
        pltpu.VMEM((CH, CH), BF16),
    ]


def learner_kernel(traj, given, torso, grad, weights, sem, *scratch):
    hs, acts = scratch[:2]
    for layer in range(2):
        clear_rim(hs.at[layer])
        clear_rim(acts.at[layer])
    copy = pltpu.make_async_copy(traj, center(hs.at[0]), sem)
    copy.start()
    weights[...] = torso[...].astype(BF16)
    copy.wait()
    learner_part(given, grad, weights, scratch, lambda half: None)


def learner(traj, given, torso):
    return pl.pallas_call(
        learner_kernel,
        out_shape=jax.ShapeDtypeStruct((TAPS, CH), F32),
        in_specs=[pl.BlockSpec(memory_space=pl.ANY), vmem(), vmem()],
        out_specs=vmem(),
        scratch_shapes=[pltpu.VMEM((2 * TAPS, CH), BF16), pltpu.SemaphoreType.DMA]
        + learner_scratch(),
        compiler_params=pltpu.CompilerParams(vmem_limit_bytes=48 << 20),
    )(traj, given, torso)


def actor_kernel(games, boards, given, torso, out, weights, sem, *scratch):
    h0, h1 = scratch[:2]
    clear_rim(h0)
    clear_rim(h1)
    start = pl.multiple_of(lax.axis_index("role") * games, games)
    copy = pltpu.make_async_copy(boards.at[:, :, pl.ds(start, games)], center(h0), sem)
    copy.start()
    weights[...] = torso[...].astype(BF16)
    copy.wait()
    actor_part(given, weights, scratch, games, out, 0, lambda layer: None)


def actor(boards, given, torso, games):
    return pl.pallas_call(
        functools.partial(actor_kernel, games),
        out_shape=jax.ShapeDtypeStruct((games, 4 * CELLS), F32),
        in_specs=[pl.BlockSpec(memory_space=pl.ANY), vmem(), vmem()],
        out_specs=vmem(),
        scratch_shapes=[pltpu.VMEM((2 * TAPS, CH), BF16), pltpu.SemaphoreType.DMA]
        + actor_scratch(games),
        compiler_params=pltpu.CompilerParams(vmem_limit_bytes=48 << 20),
    )(boards, given, torso)


def step_kernel(games, boards, traj, *refs):
    parts, (torso, moment_one, moment_two, share_out, out), scratch = refs[:7], refs[7:12], refs[12:]
    (weights, full, torso_in, one_in, two_in, grad, plane, quarter, line, norms) = scratch[:10]
    (s1, r1, s2, r2, sn, rn, sz, rz, sp, rp, ss, rs, loads, send_out, recv_out) = scratch[10:25]
    learner_refs, actor_refs = scratch[25:33], scratch[33:37]
    given, part_refs = scratch[37], scratch[38:]
    share = moment_one.shape[0]
    role = lax.axis_index("role")
    dp = lax.axis_index("dp")
    z, spot = dp // 4, dp % 4
    owner = z // 2 == role
    start = pl.multiple_of(role * games, games)

    def send(src, dst, send_sem, recv_sem, to_role, to_dp):
        copy = pltpu.make_async_remote_copy(
            src_ref=src,
            dst_ref=dst,
            send_sem=send_sem,
            recv_sem=recv_sem,
            device_id=(to_role, to_dp),
            device_id_type=MESH,
        )
        return copy

    barrier = pltpu.get_barrier_semaphore()

    def greet(to_role, to_dp):
        pl.semaphore_signal(barrier, inc=1, device_id=(to_role, to_dp), device_id_type=MESH)

    @pl.when(owner)
    def _():
        for k in range(1, 16):
            other = (dp + k) % 16
            greet(other // 8, other)
        for o in range(2):
            greet(role, (2 - 2 * role + o) * 4 + spot)
        greet(1 - role, dp)

    @pl.when(jnp.logical_not(owner))
    def _():
        for k in range(1, 4):
            greet(role, z * 4 + (spot + k) % 4)
            greet(role, ((z + k) % 4) * 4 + spot)
        greet(1 - role, dp)

    hs, acts = learner_refs[:2]
    clear_rim(hs.at[0])
    load_traj = pltpu.make_async_copy(traj, center(hs.at[0]), loads.at[0])
    load_torso = pltpu.make_async_copy(torso, torso_in, loads.at[1])
    load_one = pltpu.make_async_copy(moment_one, one_in, loads.at[2])
    load_two = pltpu.make_async_copy(moment_two, two_in, loads.at[3])
    load_torso.start()
    load_traj.start()
    clear_rim(actor_refs[0])
    load_boards = pltpu.make_async_copy(
        boards.at[:, :, pl.ds(start, games)], center(actor_refs[0]), loads.at[4]
    )
    load_parts = [
        pltpu.make_async_copy(part, ref, loads.at[5 + n])
        for n, (part, ref) in enumerate(zip(parts, part_refs))
    ]
    for load in load_parts:
        load.start()
    load_one.start()
    load_two.start()
    load_boards.start()
    clear_rim(hs.at[1])
    clear_rim(acts.at[0])
    clear_rim(acts.at[1])
    clear_rim(actor_refs[1])
    for load in load_parts:
        load.wait()
    policy_ref, value_ref, length_ref = part_refs[:3]
    given[...] = jnp.zeros(given.shape, F32)
    given[0:4, :] = policy_ref[...].astype(F32)
    given[4:5, :] = value_ref[...].astype(F32)
    given[5:6, :] = jnp.broadcast_to(length_ref[...].astype(F32), (1, CH))
    for n, ref in enumerate(part_refs[3:]):
        given[8 + n : 9 + n, 0:16] = ref[...].astype(F32)
    load_torso.wait()
    weights[...] = torso_in[...].astype(BF16)
    load_traj.wait()

    def rows(index):
        return pl.ds(pl.multiple_of(index * share, 8), share)

    def to_plane(o, k):
        p = (spot + k) % 4
        return send(
            grad.at[rows(4 * o + p)],
            plane.at[o, spot],
            s1.at[o, k - 1],
            r1.at[o, spot],
            role,
            z * 4 + p,
        )

    def from_plane(o, k):
        p = (spot + k) % 4
        return send(
            grad.at[rows(4 * o + p)], plane.at[o, p], s1.at[o, k - 1], r1.at[o, p], role, z * 4 + p
        )

    def after_half(half):
        if half == 0:

            @pl.when(owner)
            def _():
                pl.semaphore_wait(barrier, 18)

            @pl.when(jnp.logical_not(owner))
            def _():
                pl.semaphore_wait(barrier, 7)

        for k in range(1, 4):
            to_plane(half, k).start()

    learner_part(given, grad, weights, learner_refs, after_half)
    load_one.wait()
    load_two.wait()
    load_boards.wait()

    def to_owner(o):
        return send(
            quarter.at[o], line.at[z], s2.at[o], r2.at[z], role, (2 * role + o) * 4 + spot
        )

    for o in range(2):
        summed = grad[rows(4 * o + spot)]
        for k in range(1, 4):
            from_plane(o, k).wait_recv()
            summed = summed + plane[o, (spot + k) % 4]
        quarter[o] = summed

        @pl.when(z != 2 * role + o)
        def _():
            to_owner(o).start()

    def to_peer(o, k):
        p = (spot + k) % 4
        at = full.at[rows((2 * role + o) * 4 + spot)]
        return send(at, at, sp.at[o, k - 1], rp.at[o, spot], role, z * 4 + p)

    def to_sibling(o, k):
        p = (spot + k) % 4
        at = full.at[rows((2 * role + o) * 4 + p)]
        return send(at, at, ss.at[o, k], rs.at[o, p], 1 - role, dp)

    def to_norm(k):
        other = (dp + k) % 16
        return send(norms.at[dp], norms.at[dp], sn.at[k - 1], rn.at[dp], other // 8, other)

    def from_norm(k):
        other = (dp + k) % 16
        return send(norms.at[other], norms.at[other], sn.at[k - 1], rn.at[other], other // 8, other)

    def down_line(k):
        return send(
            full.at[rows(dp)],
            full.at[rows(dp)],
            sz.at[k - 1],
            rz.at[z % 2],
            role,
            ((z + k) % 4) * 4 + spot,
        )

    @pl.when(owner)
    def _():
        summed = quarter[z % 2]
        for k in range(1, 4):
            other = (z + k) % 4
            send(
                quarter.at[0], line.at[other], s2.at[0], r2.at[other], role, other * 4 + spot
            ).wait_recv()
            summed = summed + line[other]
        norms[dp] = jnp.sum((summed * summed).reshape(share // 8, 8, CH), axis=0)
        for k in range(1, 16):
            to_norm(k).start()
        for k in range(1, 16):
            from_norm(k).wait_recv()
        square_sum = jnp.sum(jnp.sum(norms[...], axis=0), axis=0, keepdims=True)
        square_sum = jnp.sum(square_sum, axis=1, keepdims=True)
        size = float(torso.shape[0] * torso.shape[1])
        factor = jnp.minimum(1.0, jnp.sqrt(jnp.full((1, 1), size, F32)) / jnp.sqrt(square_sum + NORM_EPS))
        clipped = summed * factor
        one = BETA_ONE * one_in[...] + (1.0 - BETA_ONE) * clipped
        two = BETA_TWO * two_in[...] + (1.0 - BETA_TWO) * clipped * clipped
        full[rows(dp)] = torso_in[rows(dp)] - LEARN_RATE * one / (jnp.sqrt(two) + ADAM_EPS)
        for k in range(1, 4):
            down_line(k).start()
        for k in range(1, 4):
            to_peer(z % 2, k).start()
        to_sibling(z % 2, 0).start()

    for o in range(2):
        at = full.at[rows((2 * role + o) * 4 + spot)]

        @pl.when(z != 2 * role + o)
        def _():
            send(at, at, sz.at[0], rz.at[o], role, (2 * role + o) * 4 + spot).wait_recv()
            for k in range(1, 4):
                to_peer(o, k).start()
            to_sibling(o, 0).start()

    for o in range(2):
        for k in range(1, 4):
            p = (spot + k) % 4
            at = full.at[rows((2 * role + o) * 4 + p)]
            send(at, at, sp.at[o, k - 1], rp.at[o, p], role, z * 4 + p).wait_recv()
            to_sibling(o, k).start()

    def from_sibling():
        for o in range(2):
            for p in range(4):
                at = full.at[rows((2 - 2 * role + o) * 4 + p)]
                send(at, at, ss.at[o, p], rs.at[o, p], 1 - role, dp).wait_recv()

    def ready(layer):
        @pl.when(role == 1 - layer)
        def _():
            from_sibling()

        at = slice(layer * TAPS, (layer + 1) * TAPS)
        weights[at, :] = full[at, :].astype(BF16)

    actor_part(given, weights, actor_refs, games, out, start, ready)
    share_out[...] = full[rows(dp)]
    mine = out.at[pl.ds(start, games)]
    send(mine, mine, send_out, recv_out, 1 - role, dp).start()
    theirs = out.at[pl.ds(pl.multiple_of((1 - role) * games, games), games)]
    send(mine, theirs, send_out, recv_out, 1 - role, dp).wait_recv()
    send(mine, mine, send_out, recv_out, 1 - role, dp).wait_send()
    for o in range(2):
        for k in range(1, 4):
            to_plane(o, k).wait_send()
            to_peer(o, k).wait_send()
        for k in range(4):
            to_sibling(o, k).wait_send()

        @pl.when(z != 2 * role + o)
        def _():
            to_owner(o).wait_send()

    @pl.when(owner)
    def _():
        for k in range(1, 16):
            to_norm(k).wait_send()
        for k in range(1, 4):
            down_line(k).wait_send()


def step_call(boards, traj, parts, torso, moment_one, moment_two):
    share, games = moment_one.shape[0], boards.shape[2] // 2
    dma = pltpu.SemaphoreType.DMA
    return pl.pallas_call(
        functools.partial(step_kernel, games),
        out_shape=(
            jax.ShapeDtypeStruct((share, CH), F32),
            jax.ShapeDtypeStruct((2 * games, 4 * CELLS), F32),
        ),
        in_specs=[pl.BlockSpec(memory_space=pl.ANY) for _ in range(12)],
        out_specs=(vmem(), vmem()),
        scratch_shapes=[
            pltpu.VMEM((2 * TAPS, CH), BF16),
            pltpu.VMEM((2 * TAPS, CH), F32),
            pltpu.VMEM((2 * TAPS, CH), F32),
            pltpu.VMEM((share, CH), F32),
            pltpu.VMEM((share, CH), F32),
            pltpu.VMEM((TAPS, CH), F32),
            pltpu.VMEM((2, 4, share, CH), F32),
            pltpu.VMEM((2, share, CH), F32),
            pltpu.VMEM((4, share, CH), F32),
            pltpu.VMEM((16, 8, CH), F32),
            dma((2, 3)),
            dma((2, 4)),
            dma((2,)),
            dma((4,)),
            dma((15,)),
            dma((16,)),
            dma((3,)),
            dma((2,)),
            dma((2, 3)),
            dma((2, 4)),
            dma((2, 4)),
            dma((2, 4)),
            dma((12,)),
            dma,
            dma,
        ]
        + learner_scratch()
        + actor_scratch(games)
        + [pltpu.VMEM((16, CH), F32)]
        + [pltpu.VMEM(part.shape, part.dtype) for part in parts],
        compiler_params=pltpu.CompilerParams(
            collective_id=0, has_side_effects=True, vmem_limit_bytes=56 << 20
        ),
    )(boards, traj, *parts, torso, moment_one, moment_two)


def update_any(grad, torso, moment_one, moment_two):
    share = moment_one.shape[0]
    summed = lax.all_gather(lax.psum(grad, "dp"), "role", axis=0, tiled=True)
    start = lax.axis_index("dp") * share
    square_sum = jnp.sum(summed * summed)
    factor = jnp.minimum(1.0, jnp.sqrt(float(summed.size)) / jnp.sqrt(square_sum + NORM_EPS))
    clipped = lax.dynamic_slice_in_dim(summed, start, share, 0) * factor
    one = BETA_ONE * moment_one + (1.0 - BETA_ONE) * clipped
    two = BETA_TWO * moment_two + (1.0 - BETA_TWO) * clipped * clipped
    old = lax.dynamic_slice_in_dim(torso, start, share, 0)
    new = old - LEARN_RATE * one / (jnp.sqrt(two) + ADAM_EPS)
    return lax.all_gather(new, "dp", axis=0, tiled=True)


def join_kernel(part, out, send_sem, recv_sem):
    games = part.shape[0]
    role = lax.axis_index("role")
    dp = lax.axis_index("dp")
    barrier = pltpu.get_barrier_semaphore()
    pl.semaphore_signal(barrier, inc=1, device_id=(1 - role, dp), device_id_type=MESH)
    pl.semaphore_wait(barrier, 1)
    mine = pl.ds(pl.multiple_of(role * games, 8), games)
    copy = pltpu.make_async_remote_copy(
        src_ref=part,
        dst_ref=out.at[mine],
        send_sem=send_sem,
        recv_sem=recv_sem,
        device_id=(1 - role, dp),
        device_id_type=MESH,
    )
    copy.start()
    out[mine] = part[...]
    copy.wait()


def join(part):
    return pl.pallas_call(
        join_kernel,
        out_shape=jax.ShapeDtypeStruct((2 * part.shape[0], part.shape[1]), F32),
        in_specs=[vmem()],
        out_specs=vmem(),
        scratch_shapes=[pltpu.SemaphoreType.DMA, pltpu.SemaphoreType.DMA],
        compiler_params=pltpu.CompilerParams(collective_id=1, has_side_effects=True),
    )(part)


def body(
    board_now,
    traj_boards,
    actions,
    lengths,
    behaviour,
    regular,
    rewards,
    torso,
    policy_head,
    value_head,
    first_moment,
    second_moment,
):
    boards = jnp.transpose(board_now, (1, 2, 0, 3))
    traj = jnp.transpose(traj_boards[0], (1, 2, 0, 3))
    if lax.axis_size("dp") == 16 and lax.axis_size("role") == 2:
        parts = (policy_head.T, value_head[None, :], lengths[:, None])
        parts = parts + (actions, behaviour, regular, rewards)
        return step_call(boards, traj, parts, torso, first_moment, second_moment)

    def wide(x):
        return jnp.pad(x.astype(F32), ((0, 0), (0, CH - x.shape[1])))

    given = jnp.concatenate(
        [
            policy_head.T.astype(F32),
            value_head[None, :].astype(F32),
            jnp.broadcast_to(lengths.astype(F32)[:, None], (1, CH)),
            jnp.zeros((2, CH), F32),
            wide(actions),
            wide(behaviour),
            wide(regular),
            wide(rewards),
            jnp.zeros((4, CH), F32),
        ],
        axis=0,
    )
    grad = learner(traj, given, torso)
    weights = update_any(grad, torso, first_moment, second_moment)
    share_rows = first_moment.shape[0]
    start = lax.axis_index("dp") * share_rows
    new_share = lax.dynamic_slice_in_dim(weights, start, share_rows, 0)
    part = actor(boards, given, weights, board_now.shape[0] // 2)
    return (new_share, join(part))


def solution(mesh):
    return jax.shard_map(
        body,
        mesh=mesh,
        in_specs=(
            P("dp", None, None, None),
            P("dp", None, None, None, None),
            P("dp", None),
            P("dp"),
            P("dp", None),
            P("dp", None),
            P("dp", None),
            P(),
            P(),
            P(),
            P("dp", None),
            P("dp", None),
        ),
        out_specs=(P("dp", None), P("dp", None)),
        check_vma=False,
    )
```

```python
import functools

import jax
import jax.numpy as jnp
from jax import lax
from jax.experimental import pallas as pl
from jax.experimental.pallas import tpu as pltpu
from jax.sharding import PartitionSpec as P

ETA = 0.2
LEARN_RATE = 0.03
BETA_ONE = 0.9
BETA_TWO = 0.999
ADAM_EPS = 1e-08
NORM_EPS = 1e-12
SIDE = 10
CELLS = 100
CH = 128
TAPS = 9 * CH
PACKED = 12 * CH
ROWS = 5
F32 = jnp.float32
BF16 = jnp.bfloat16
MESH = pl.DeviceIdType.MESH


def vmem():
    return pl.BlockSpec(memory_space=pltpu.VMEM)


def columns(padded, i, games, flip, first=0, last=9):
    parts = []
    for offset in range(first, last):
        p, q = offset // 3, offset % 3
        u, v = (2 - p, 2 - q) if flip else (p, q)
        window = padded[pl.ds(i + u, ROWS), v : v + SIDE]
        parts.append(window.reshape(ROWS * SIDE * games, CH))
    return jnp.concatenate(parts, axis=1)


def pair_columns(padded, i, games):
    parts = []
    for p in range(3):
        for u in range(4):
            cells = [
                padded[pl.ds(i + p, ROWS), u + 2 * m : u + 2 * m + 1] for m in range(SIDE // 2)
            ]
            parts.append(jnp.concatenate(cells, axis=1).reshape(ROWS * SIDE // 2 * games, CH))
    return jnp.concatenate(parts, axis=1)


def pair_dot(padded, i, games, packed):
    both = jnp.dot(pair_columns(padded, i, games), packed, preferred_element_type=F32)
    shape = (ROWS, SIDE // 2, 1, games, CH)
    halves = [both[:, 0:CH].reshape(shape), both[:, CH : 2 * CH].reshape(shape)]
    return jnp.concatenate(halves, axis=2).reshape(ROWS * SIDE * games, CH)


def pack(packed, blocks, back=False):
    for offset in range(9):
        p, q = offset // 3, offset % 3
        block = blocks(offset)
        for cell in range(2):
            row, u = (2 - p, cell + 2 - q) if back else (p, q + cell)
            at = (row * 4 + u) * CH
            packed[at : at + CH, cell * CH : (cell + 1) * CH] = block


def pack_layer(weights, torso, layer):
    def block(offset):
        at = layer * TAPS + offset * CH
        return torso[at : at + CH, :].astype(BF16)

    pack(weights.at[layer], block)


def inner(padded, i, games):
    return padded[pl.ds(i + 1, ROWS), 1 : 1 + SIDE].reshape(ROWS * SIDE * games, CH)


def set_inner(padded, i, games, value):
    padded[pl.ds(i + 1, ROWS), 1 : 1 + SIDE] = value.reshape(ROWS, SIDE, games, CH)


def clear_rim(padded):
    zero = jnp.zeros((1, SIDE + 2) + padded.shape[2:], padded.dtype)
    side = jnp.zeros((SIDE, 1) + padded.shape[2:], padded.dtype)
    padded[0:1] = zero
    padded[SIDE + 1 : SIDE + 2] = zero
    padded[1 : SIDE + 1, 0:1] = side
    padded[1 : SIDE + 1, SIDE + 1 : SIDE + 2] = side


def center(padded):
    return padded.at[pl.ds(1, SIDE), pl.ds(1, SIDE)]


def steps(f):
    for step in range(SIDE // ROWS):
        f(step, step * ROWS)


def lane_sum(x, games):
    shift = 64
    while shift >= games:
        x = x + pltpu.roll(x, shift, 1)
        shift //= 2
    return x


def spread_heads(given, games, amount):
    rows = [jnp.broadcast_to(given[d : d + 1, :], (games, CH)) for d in range(amount)]
    if games * amount < CH:
        rows.append(jnp.zeros((CH - games * amount, CH), F32))
    return jnp.concatenate(rows, axis=0).astype(BF16)


def own_lane(games):
    game = lax.broadcasted_iota(jnp.int32, (games, CH), 0)
    lane = lax.broadcasted_iota(jnp.int32, (games, CH), 1)
    return (lane % games == game).astype(F32)


def head_cells(h, heads, mine, games):
    out = lax.dot_general(h, heads[...], (((1,), (1,)), ((), ())), preferred_element_type=F32)
    return jnp.sum(out.reshape(ROWS * SIDE, games, CH) * mine[None], axis=1)


def advance(source, i, games, layer_weights):
    act = pair_dot(source, i, games, layer_weights[...])
    return act, (inner(source, i, games).astype(F32) + jnp.maximum(act, 0.0)).astype(BF16)


def trace_terms(logits_ref, given, games):
    spread = lane_sum(given[8:16], games)
    action = spread[0:1].astype(jnp.int32)
    behave, regul, reward = spread[1:2], spread[2:3], spread[3:4]
    lane = lax.broadcasted_iota(jnp.int32, (1, CH), 1)
    slot = lane % games
    every = logits_ref[...]
    cell_id = lax.broadcasted_iota(jnp.int32, every.shape, 0) * SIDE + lax.broadcasted_iota(
        jnp.int32, every.shape, 1
    )
    lane_full = lax.broadcasted_iota(jnp.int32, every.shape, 2)
    policy_full = lane_full < 4 * games
    taken = (lane_full // games) * CELLS + cell_id == action.reshape(1, 1, CH)
    taken = jnp.where(policy_full, jnp.where(taken, 1.0, 0.0), 0.0)
    logits = jnp.where(policy_full, every, 0.0)

    def over_cells(x):
        return jnp.sum(jnp.sum(x, axis=0), axis=0, keepdims=True)

    exps = jnp.where(policy_full, jnp.exp(logits), 0.0)
    log_total = jnp.log(lane_sum(over_cells(exps), games))
    logp = lane_sum(over_cells(taken * logits), games) - log_total
    value_lane = jnp.where((lane >= 4 * games) & (lane < 5 * games), 1.0, 0.0)
    values = jnp.tanh(lane_sum(over_cells(every) * value_lane, games) / CELLS)

    def ahead(x, by):
        return jnp.where(slot + by < games, pltpu.roll(x, CH - by, 1), 0.0)

    length = given[5:6]
    place = slot.astype(F32)
    live = jnp.where(place < length, 1.0, 0.0)
    next_live = jnp.where(place + 1.0 < length, 1.0, 0.0)
    ratio = jnp.minimum(1.0, jnp.exp(logp - behave))
    shaped = reward - ETA * (logp - regul)
    delta = live * ratio * (shaped + ahead(values, 1) * next_live - values)
    correction, slope = live * delta, live * ratio
    by = 1
    while by < games:
        correction = correction + slope * ahead(correction, by)
        slope = slope * ahead(slope, by)
        by *= 2
    targets = values + correction
    policy_term = -live * ratio * (shaped + ahead(targets, 1) * next_live - values)
    value_term = -live * (targets - values)
    value_cell = value_term * (1.0 - values * values) / CELLS * value_lane
    probs = jnp.exp(logits - log_total.reshape(1, 1, CH))
    logits_ref[...] = jnp.where(
        policy_full,
        policy_term.reshape(1, 1, CH) * (taken - probs),
        jnp.broadcast_to(value_cell.reshape(1, 1, CH), logits.shape),
    )


def learner_part(given, torso, grad, weights, scratch, after_half):
    hs, acts, turned, pre, hidden_grad, cells, heads, total = scratch
    games = 16
    size = ROWS * SIDE * games
    role = lax.axis_index("role")
    h0, h1, a0, a1 = hs.at[0], hs.at[1], acts.at[0], acts.at[1]
    heads[...] = spread_heads(given, games, 5)
    mine = own_lane(games)

    def layer_one(step, i):
        act, h = advance(h0, i, games, weights.at[0])
        pre[0, pl.ds(step * size, size)] = act
        set_inner(h1, i, games, h)

    steps(layer_one)

    def layer_two(step, i):
        act, h = advance(h1, i, games, weights.at[1])
        pre[1, pl.ds(step * size, size)] = act
        cells[pl.ds(i, ROWS)] = head_cells(h, heads, mine, games).reshape(ROWS, SIDE, CH)

    steps(layer_two)
    trace_terms(cells, given, games)

    def top(step, i):
        at = pl.ds(step * size, size)
        g = cells[pl.ds(i, ROWS)].reshape(ROWS * SIDE, 1, CH) * mine[None]
        g = g.reshape(size, CH)
        high = g.astype(BF16)
        low = (g - high.astype(F32)).astype(BF16)
        out = jnp.dot(high, heads[...], preferred_element_type=F32)
        out = out + jnp.dot(low, heads[...], preferred_element_type=F32)
        hidden_grad[at] = out
        set_inner(a1, i, games, jnp.where(pre[1, at] > 0, out, 0.0).astype(BF16))

    steps(top)

    @pl.when(role == 0)
    def _():
        turned[...] = jnp.zeros(turned.shape, BF16)

        def block(offset):
            at = TAPS + offset * CH
            return torso[at : at + CH, :].T.astype(BF16)

        pack(turned, block, True)

        def back(step, i):
            at = pl.ds(step * size, size)
            out = hidden_grad[at] + pair_dot(a1, i, games, turned[...])
            set_inner(a0, i, games, jnp.where(pre[0, at] > 0, out, 0.0).astype(BF16))

        steps(back)

    h, a = hs.at[role], acts.at[role]
    for half, (first, last) in enumerate(((0, 5), (5, 9))):
        lanes = slice(first * CH, last * CH)

        def product(i):
            return lax.dot_general(
                inner(h, i, games),
                columns(a, i, games, True, first, last),
                (((0,), (0,)), ((), ())),
                preferred_element_type=F32,
            )

        summed = product(0)
        for step in range(1, SIDE // ROWS):
            summed = summed + product(step * ROWS)
        for offset in range(first, last):
            at = (offset - first) * CH
            grad[offset * CH : (offset + 1) * CH, :] = summed[:, at : at + CH]
        after_half(half)


def learner_scratch():
    padded = (2, SIDE + 2, SIDE + 2, 16, CH)
    return [
        pltpu.VMEM(padded, BF16),
        pltpu.VMEM(padded, BF16),
        pltpu.VMEM((PACKED, 2 * CH), BF16),
        pltpu.VMEM((2, 1600, CH), F32),
        pltpu.VMEM((1600, CH), F32),
        pltpu.VMEM((SIDE, SIDE, CH), F32),
        pltpu.VMEM((CH, CH), BF16),
        pltpu.VMEM((8, CH), F32),
    ]


def actor_part(given, weights, scratch, games, out, start, ready):
    h0, h1, cells, heads = scratch
    heads[...] = spread_heads(given, games, 4)
    cells[...] = jnp.zeros(cells.shape, F32)
    mine = own_lane(games)
    ready(0)

    def layer_one(step, i):
        _, h = advance(h0, i, games, weights.at[0])
        set_inner(h1, i, games, h)

    steps(layer_one)
    ready(1)

    def layer_two(step, i):
        _, h = advance(h1, i, games, weights.at[1])
        found = head_cells(h, heads, mine, games).reshape(ROWS, SIDE, CH)
        for part in range(ROWS):
            cells[pl.ds((i + part) * SIDE, SIDE), :] = found[part]

    steps(layer_two)
    logits = cells[...]
    cell_id = lax.broadcasted_iota(jnp.int32, logits.shape, 0)
    exps = jnp.where(cell_id < CELLS, jnp.exp(logits), 0.0)
    log_total = jnp.log(lane_sum(jnp.sum(exps, axis=0, keepdims=True), games))
    turned = (logits - log_total).T
    for d in range(4):
        out[pl.ds(start, games), d * CELLS : (d + 1) * CELLS] = turned[
            d * games : (d + 1) * games, 0:CELLS
        ]


def actor_scratch(games):
    padded = (SIDE + 2, SIDE + 2, games, CH)
    return [
        pltpu.VMEM(padded, BF16),
        pltpu.VMEM(padded, BF16),
        pltpu.VMEM((CH, CH), F32),
        pltpu.VMEM((CH, CH), BF16),
    ]


def learner_kernel(traj, given, torso, grad, weights, sem, *scratch):
    hs, acts = scratch[:2]
    for layer in range(2):
        clear_rim(hs.at[layer])
        clear_rim(acts.at[layer])
    copy = pltpu.make_async_copy(traj, center(hs.at[0]), sem)
    copy.start()
    weights[...] = jnp.zeros(weights.shape, BF16)
    for layer in range(2):
        pack_layer(weights, torso, layer)
    copy.wait()
    learner_part(given, torso, grad, weights, scratch, lambda half: None)


def learner(traj, given, torso):
    return pl.pallas_call(
        learner_kernel,
        out_shape=jax.ShapeDtypeStruct((TAPS, CH), F32),
        in_specs=[pl.BlockSpec(memory_space=pl.ANY), vmem(), vmem()],
        out_specs=vmem(),
        scratch_shapes=[pltpu.VMEM((2, PACKED, 2 * CH), BF16), pltpu.SemaphoreType.DMA]
        + learner_scratch(),
        compiler_params=pltpu.CompilerParams(vmem_limit_bytes=48 << 20),
    )(traj, given, torso)


def actor_kernel(games, boards, given, torso, out, weights, sem, *scratch):
    h0, h1 = scratch[:2]
    clear_rim(h0)
    clear_rim(h1)
    start = pl.multiple_of(lax.axis_index("role") * games, games)
    copy = pltpu.make_async_copy(boards.at[:, :, pl.ds(start, games)], center(h0), sem)
    copy.start()
    weights[...] = jnp.zeros(weights.shape, BF16)
    for layer in range(2):
        pack_layer(weights, torso, layer)
    copy.wait()
    actor_part(given, weights, scratch, games, out, 0, lambda layer: None)


def actor(boards, given, torso, games):
    return pl.pallas_call(
        functools.partial(actor_kernel, games),
        out_shape=jax.ShapeDtypeStruct((games, 4 * CELLS), F32),
        in_specs=[pl.BlockSpec(memory_space=pl.ANY), vmem(), vmem()],
        out_specs=vmem(),
        scratch_shapes=[pltpu.VMEM((2, PACKED, 2 * CH), BF16), pltpu.SemaphoreType.DMA]
        + actor_scratch(games),
        compiler_params=pltpu.CompilerParams(vmem_limit_bytes=48 << 20),
    )(boards, given, torso)


def step_kernel(games, boards, traj, *refs):
    parts, (torso, moment_one, moment_two, share_out, out), scratch = refs[:7], refs[7:12], refs[12:]
    (weights, full, torso_in, one_in, two_in, grad, plane, quarter, line, norms) = scratch[:10]
    (s1, r1, s2, r2, sn, rn, sz, rz, sp, rp, ss, rs, loads, send_out, recv_out) = scratch[10:25]
    learner_refs, actor_refs = scratch[25:33], scratch[33:37]
    given, part_refs = scratch[37], scratch[38:]
    share = moment_one.shape[0]
    role = lax.axis_index("role")
    dp = lax.axis_index("dp")
    z, spot = dp // 4, dp % 4
    owner = z // 2 == role
    start = pl.multiple_of(role * games, games)

    def send(src, dst, send_sem, recv_sem, to_role, to_dp):
        copy = pltpu.make_async_remote_copy(
            src_ref=src,
            dst_ref=dst,
            send_sem=send_sem,
            recv_sem=recv_sem,
            device_id=(to_role, to_dp),
            device_id_type=MESH,
        )
        return copy

    barrier = pltpu.get_barrier_semaphore()

    def greet(to_role, to_dp):
        pl.semaphore_signal(barrier, inc=1, device_id=(to_role, to_dp), device_id_type=MESH)

    @pl.when(owner)
    def _():
        for k in range(1, 16):
            other = (dp + k) % 16
            greet(other // 8, other)
        for o in range(2):
            greet(role, (2 - 2 * role + o) * 4 + spot)
        greet(1 - role, dp)

    @pl.when(jnp.logical_not(owner))
    def _():
        for k in range(1, 4):
            greet(role, z * 4 + (spot + k) % 4)
            greet(role, ((z + k) % 4) * 4 + spot)
        greet(1 - role, dp)

    hs, acts = learner_refs[:2]
    clear_rim(hs.at[0])
    load_traj = pltpu.make_async_copy(traj, center(hs.at[0]), loads.at[0])
    load_torso = pltpu.make_async_copy(torso, torso_in, loads.at[1])
    load_one = pltpu.make_async_copy(moment_one, one_in, loads.at[2])
    load_two = pltpu.make_async_copy(moment_two, two_in, loads.at[3])
    load_torso.start()
    load_traj.start()
    clear_rim(actor_refs[0])
    load_boards = pltpu.make_async_copy(
        boards.at[:, :, pl.ds(start, games)], center(actor_refs[0]), loads.at[4]
    )
    load_parts = [
        pltpu.make_async_copy(part, ref, loads.at[5 + n])
        for n, (part, ref) in enumerate(zip(parts, part_refs))
    ]
    for load in load_parts:
        load.start()
    load_one.start()
    load_two.start()
    load_boards.start()
    clear_rim(hs.at[1])
    clear_rim(acts.at[0])
    clear_rim(acts.at[1])
    clear_rim(actor_refs[1])
    for load in load_parts:
        load.wait()
    policy_ref, value_ref, length_ref = part_refs[:3]
    given[...] = jnp.zeros(given.shape, F32)
    given[0:4, :] = policy_ref[...].astype(F32)
    given[4:5, :] = value_ref[...].astype(F32)
    given[5:6, :] = jnp.broadcast_to(length_ref[...].astype(F32), (1, CH))
    for n, ref in enumerate(part_refs[3:]):
        given[8 + n : 9 + n, 0:16] = ref[...].astype(F32)
    weights[...] = jnp.zeros(weights.shape, BF16)
    load_torso.wait()
    for layer in range(2):
        pack_layer(weights, torso_in, layer)
    load_traj.wait()

    def rows(index):
        return pl.ds(pl.multiple_of(index * share, 8), share)

    def to_plane(o, k):
        p = (spot + k) % 4
        return send(
            grad.at[rows(4 * o + p)],
            plane.at[o, spot],
            s1.at[o, k - 1],
            r1.at[o, spot],
            role,
            z * 4 + p,
        )

    def from_plane(o, k):
        p = (spot + k) % 4
        return send(
            grad.at[rows(4 * o + p)], plane.at[o, p], s1.at[o, k - 1], r1.at[o, p], role, z * 4 + p
        )

    def after_half(half):
        if half == 0:

            @pl.when(owner)
            def _():
                pl.semaphore_wait(barrier, 18)

            @pl.when(jnp.logical_not(owner))
            def _():
                pl.semaphore_wait(barrier, 7)

        for k in range(1, 4):
            to_plane(half, k).start()

    learner_part(given, torso_in, grad, weights, learner_refs, after_half)
    load_one.wait()
    load_two.wait()
    load_boards.wait()

    def to_owner(o):
        return send(
            quarter.at[o], line.at[z], s2.at[o], r2.at[z], role, (2 * role + o) * 4 + spot
        )

    for o in range(2):
        summed = grad[rows(4 * o + spot)]
        for k in range(1, 4):
            from_plane(o, k).wait_recv()
            summed = summed + plane[o, (spot + k) % 4]
        quarter[o] = summed

        @pl.when(z != 2 * role + o)
        def _():
            to_owner(o).start()

    def to_peer(o, k):
        p = (spot + k) % 4
        at = full.at[rows((2 * role + o) * 4 + spot)]
        return send(at, at, sp.at[o, k - 1], rp.at[o, spot], role, z * 4 + p)

    def to_sibling(o, k):
        p = (spot + k) % 4
        at = full.at[rows((2 * role + o) * 4 + p)]
        return send(at, at, ss.at[o, k], rs.at[o, p], 1 - role, dp)

    def to_norm(k):
        other = (dp + k) % 16
        return send(norms.at[dp], norms.at[dp], sn.at[k - 1], rn.at[dp], other // 8, other)

    def from_norm(k):
        other = (dp + k) % 16
        return send(norms.at[other], norms.at[other], sn.at[k - 1], rn.at[other], other // 8, other)

    def down_line(k):
        return send(
            full.at[rows(dp)],
            full.at[rows(dp)],
            sz.at[k - 1],
            rz.at[z % 2],
            role,
            ((z + k) % 4) * 4 + spot,
        )

    @pl.when(owner)
    def _():
        summed = quarter[z % 2]
        for k in range(1, 4):
            other = (z + k) % 4
            send(
                quarter.at[0], line.at[other], s2.at[0], r2.at[other], role, other * 4 + spot
            ).wait_recv()
            summed = summed + line[other]
        norms[dp] = jnp.sum((summed * summed).reshape(share // 8, 8, CH), axis=0)
        for k in range(1, 16):
            to_norm(k).start()
        for k in range(1, 16):
            from_norm(k).wait_recv()
        square_sum = jnp.sum(jnp.sum(norms[...], axis=0), axis=0, keepdims=True)
        square_sum = jnp.sum(square_sum, axis=1, keepdims=True)
        size = float(torso.shape[0] * torso.shape[1])
        factor = jnp.minimum(1.0, jnp.sqrt(jnp.full((1, 1), size, F32)) / jnp.sqrt(square_sum + NORM_EPS))
        clipped = summed * factor
        one = BETA_ONE * one_in[...] + (1.0 - BETA_ONE) * clipped
        two = BETA_TWO * two_in[...] + (1.0 - BETA_TWO) * clipped * clipped
        full[rows(dp)] = torso_in[rows(dp)] - LEARN_RATE * one / (jnp.sqrt(two) + ADAM_EPS)
        for k in range(1, 4):
            down_line(k).start()
        for k in range(1, 4):
            to_peer(z % 2, k).start()
        to_sibling(z % 2, 0).start()

    for o in range(2):
        at = full.at[rows((2 * role + o) * 4 + spot)]

        @pl.when(z != 2 * role + o)
        def _():
            send(at, at, sz.at[0], rz.at[o], role, (2 * role + o) * 4 + spot).wait_recv()
            for k in range(1, 4):
                to_peer(o, k).start()
            to_sibling(o, 0).start()

    for o in range(2):
        for k in range(1, 4):
            p = (spot + k) % 4
            at = full.at[rows((2 * role + o) * 4 + p)]
            send(at, at, sp.at[o, k - 1], rp.at[o, p], role, z * 4 + p).wait_recv()
            to_sibling(o, k).start()

    def from_sibling():
        for o in range(2):
            for p in range(4):
                at = full.at[rows((2 - 2 * role + o) * 4 + p)]
                send(at, at, ss.at[o, p], rs.at[o, p], 1 - role, dp).wait_recv()

    def ready(layer):
        @pl.when(role == 1 - layer)
        def _():
            from_sibling()

        pack_layer(weights, full, layer)

    actor_part(given, weights, actor_refs, games, out, start, ready)
    share_out[0:share] = full[rows(dp)]
    share_out[share : share + 8] = jnp.zeros((8, CH), F32)
    out[2 * games : 2 * games + 8] = jnp.zeros((8, 4 * CELLS), F32)
    mine = out.at[pl.ds(start, games)]
    send(mine, mine, send_out, recv_out, 1 - role, dp).start()
    theirs = out.at[pl.ds(pl.multiple_of((1 - role) * games, games), games)]
    send(mine, theirs, send_out, recv_out, 1 - role, dp).wait_recv()
    send(mine, mine, send_out, recv_out, 1 - role, dp).wait_send()
    for o in range(2):
        for k in range(1, 4):
            to_plane(o, k).wait_send()
            to_peer(o, k).wait_send()
        for k in range(4):
            to_sibling(o, k).wait_send()

        @pl.when(z != 2 * role + o)
        def _():
            to_owner(o).wait_send()

    @pl.when(owner)
    def _():
        for k in range(1, 16):
            to_norm(k).wait_send()
        for k in range(1, 4):
            down_line(k).wait_send()


def step_call(boards, traj, parts, torso, moment_one, moment_two):
    share, games = moment_one.shape[0], boards.shape[2] // 2
    dma = pltpu.SemaphoreType.DMA
    return pl.pallas_call(
        functools.partial(step_kernel, games),
        out_shape=(
            jax.ShapeDtypeStruct((share + 8, CH), F32),
            jax.ShapeDtypeStruct((2 * games + 8, 4 * CELLS), F32),
        ),
        in_specs=[pl.BlockSpec(memory_space=pl.ANY) for _ in range(12)],
        out_specs=(vmem(), vmem()),
        scratch_shapes=[
            pltpu.VMEM((2, PACKED, 2 * CH), BF16),
            pltpu.VMEM((2 * TAPS, CH), F32),
            pltpu.VMEM((2 * TAPS, CH), F32),
            pltpu.VMEM((share, CH), F32),
            pltpu.VMEM((share, CH), F32),
            pltpu.VMEM((TAPS, CH), F32),
            pltpu.VMEM((2, 4, share, CH), F32),
            pltpu.VMEM((2, share, CH), F32),
            pltpu.VMEM((4, share, CH), F32),
            pltpu.VMEM((16, 8, CH), F32),
            dma((2, 3)),
            dma((2, 4)),
            dma((2,)),
            dma((4,)),
            dma((15,)),
            dma((16,)),
            dma((3,)),
            dma((2,)),
            dma((2, 3)),
            dma((2, 4)),
            dma((2, 4)),
            dma((2, 4)),
            dma((12,)),
            dma,
            dma,
        ]
        + learner_scratch()
        + actor_scratch(games)
        + [pltpu.VMEM((16, CH), F32)]
        + [pltpu.VMEM(part.shape, part.dtype) for part in parts],
        compiler_params=pltpu.CompilerParams(
            collective_id=0, has_side_effects=True, vmem_limit_bytes=56 << 20
        ),
    )(boards, traj, *parts, torso, moment_one, moment_two)


def update_any(grad, torso, moment_one, moment_two):
    share = moment_one.shape[0]
    summed = lax.all_gather(lax.psum(grad, "dp"), "role", axis=0, tiled=True)
    start = lax.axis_index("dp") * share
    square_sum = jnp.sum(summed * summed)
    factor = jnp.minimum(1.0, jnp.sqrt(float(summed.size)) / jnp.sqrt(square_sum + NORM_EPS))
    clipped = lax.dynamic_slice_in_dim(summed, start, share, 0) * factor
    one = BETA_ONE * moment_one + (1.0 - BETA_ONE) * clipped
    two = BETA_TWO * moment_two + (1.0 - BETA_TWO) * clipped * clipped
    old = lax.dynamic_slice_in_dim(torso, start, share, 0)
    new = old - LEARN_RATE * one / (jnp.sqrt(two) + ADAM_EPS)
    return lax.all_gather(new, "dp", axis=0, tiled=True)


def join_kernel(part, out, send_sem, recv_sem):
    games = part.shape[0]
    role = lax.axis_index("role")
    dp = lax.axis_index("dp")
    barrier = pltpu.get_barrier_semaphore()
    pl.semaphore_signal(barrier, inc=1, device_id=(1 - role, dp), device_id_type=MESH)
    pl.semaphore_wait(barrier, 1)
    mine = pl.ds(pl.multiple_of(role * games, 8), games)
    copy = pltpu.make_async_remote_copy(
        src_ref=part,
        dst_ref=out.at[mine],
        send_sem=send_sem,
        recv_sem=recv_sem,
        device_id=(1 - role, dp),
        device_id_type=MESH,
    )
    copy.start()
    out[mine] = part[...]
    copy.wait()


def join(part):
    return pl.pallas_call(
        join_kernel,
        out_shape=jax.ShapeDtypeStruct((2 * part.shape[0], part.shape[1]), F32),
        in_specs=[vmem()],
        out_specs=vmem(),
        scratch_shapes=[pltpu.SemaphoreType.DMA, pltpu.SemaphoreType.DMA],
        compiler_params=pltpu.CompilerParams(collective_id=1, has_side_effects=True),
    )(part)


def body(
    board_now,
    traj_boards,
    actions,
    lengths,
    behaviour,
    regular,
    rewards,
    torso,
    policy_head,
    value_head,
    first_moment,
    second_moment,
):
    boards = jnp.transpose(board_now, (1, 2, 0, 3))
    traj = jnp.transpose(traj_boards[0], (1, 2, 0, 3))
    if lax.axis_size("dp") == 16 and lax.axis_size("role") == 2:
        parts = (policy_head.T, value_head[None, :], lengths[:, None])
        parts = parts + (actions, behaviour, regular, rewards)
        new_share, logp = step_call(boards, traj, parts, torso, first_moment, second_moment)
        return (new_share[: first_moment.shape[0]], logp[: board_now.shape[0]])

    def wide(x):
        return jnp.pad(x.astype(F32), ((0, 0), (0, CH - x.shape[1])))

    given = jnp.concatenate(
        [
            policy_head.T.astype(F32),
            value_head[None, :].astype(F32),
            jnp.broadcast_to(lengths.astype(F32)[:, None], (1, CH)),
            jnp.zeros((2, CH), F32),
            wide(actions),
            wide(behaviour),
            wide(regular),
            wide(rewards),
            jnp.zeros((4, CH), F32),
        ],
        axis=0,
    )
    grad = learner(traj, given, torso)
    weights = update_any(grad, torso, first_moment, second_moment)
    share_rows = first_moment.shape[0]
    start = lax.axis_index("dp") * share_rows
    new_share = lax.dynamic_slice_in_dim(weights, start, share_rows, 0)
    part = actor(boards, given, weights, board_now.shape[0] // 2)
    return (new_share, join(part))


def solution(mesh):
    return jax.shard_map(
        body,
        mesh=mesh,
        in_specs=(
            P("dp", None, None, None),
            P("dp", None, None, None, None),
            P("dp", None),
            P("dp"),
            P("dp", None),
            P("dp", None),
            P("dp", None),
            P(),
            P(),
            P(),
            P("dp", None),
            P("dp", None),
        ),
        out_specs=(P("dp", None), P("dp", None)),
        check_vma=False,
    )
```

```python
import functools

import jax
import jax.numpy as jnp
from jax import lax
from jax.experimental import pallas as pl
from jax.experimental.pallas import tpu as pltpu
from jax.sharding import PartitionSpec as P

ETA = 0.2
LEARN_RATE = 0.03
BETA_ONE = 0.9
BETA_TWO = 0.999
ADAM_EPS = 1e-08
NORM_EPS = 1e-12
SIDE = 10
CELLS = 100
CH = 128
TAPS = 9 * CH
PACKED = 12 * CH
ROWS = 5
F32 = jnp.float32
BF16 = jnp.bfloat16
MESH = pl.DeviceIdType.MESH


def vmem():
    return pl.BlockSpec(memory_space=pltpu.VMEM)


def pair_columns(padded, i, games):
    parts = []
    for p in range(3):
        for u in range(4):
            cells = [
                padded[pl.ds(i + p, ROWS), u + 2 * m : u + 2 * m + 1] for m in range(SIDE // 2)
            ]
            parts.append(jnp.concatenate(cells, axis=1).reshape(ROWS * SIDE // 2 * games, CH))
    return jnp.concatenate(parts, axis=1)


def pair_dot(padded, i, games, packed):
    both = jnp.dot(pair_columns(padded, i, games), packed, preferred_element_type=F32)
    shape = (ROWS, SIDE // 2, 1, games, CH)
    halves = [both[:, 0:CH].reshape(shape), both[:, CH : 2 * CH].reshape(shape)]
    return jnp.concatenate(halves, axis=2).reshape(ROWS * SIDE * games, CH)


def pack(packed, blocks, back=False):
    for offset in range(9):
        p, q = offset // 3, offset % 3
        block = blocks(offset)
        for cell in range(2):
            row, u = (2 - p, cell + 2 - q) if back else (p, q + cell)
            at = (row * 4 + u) * CH
            packed[at : at + CH, cell * CH : (cell + 1) * CH] = block


def pack_layer(weights, torso, layer):
    def block(offset):
        at = layer * TAPS + offset * CH
        return torso[at : at + CH, :].astype(BF16)

    pack(weights.at[layer], block)


def inner(padded, i, games):
    return padded[pl.ds(i + 1, ROWS), 1 : 1 + SIDE].reshape(ROWS * SIDE * games, CH)


def set_inner(padded, i, games, value):
    padded[pl.ds(i + 1, ROWS), 1 : 1 + SIDE] = value.reshape(ROWS, SIDE, games, CH)


def clear_rim(padded):
    zero = jnp.zeros((1, SIDE + 2) + padded.shape[2:], padded.dtype)
    side = jnp.zeros((SIDE, 1) + padded.shape[2:], padded.dtype)
    padded[0:1] = zero
    padded[SIDE + 1 : SIDE + 2] = zero
    padded[1 : SIDE + 1, 0:1] = side
    padded[1 : SIDE + 1, SIDE + 1 : SIDE + 2] = side


def center(padded):
    return padded.at[pl.ds(1, SIDE), pl.ds(1, SIDE)]


def steps(f):
    for step in range(SIDE // ROWS):
        f(step, step * ROWS)


def lane_sum(x, games):
    shift = 64
    while shift >= games:
        x = x + pltpu.roll(x, shift, 1)
        shift //= 2
    return x


def spread_heads(given, games, amount):
    rows = [jnp.broadcast_to(given[d : d + 1, :], (games, CH)) for d in range(amount)]
    if games * amount < CH:
        rows.append(jnp.zeros((CH - games * amount, CH), F32))
    return jnp.concatenate(rows, axis=0).astype(BF16)


def own_lane(games):
    game = lax.broadcasted_iota(jnp.int32, (games, CH), 0)
    lane = lax.broadcasted_iota(jnp.int32, (games, CH), 1)
    return (lane % games == game).astype(F32)


def head_cells(h, heads, mine, games):
    out = lax.dot_general(h, heads[...], (((1,), (1,)), ((), ())), preferred_element_type=F32)
    return jnp.sum(out.reshape(ROWS * SIDE, games, CH) * mine[None], axis=1)


def advance(source, i, games, layer_weights):
    act = pair_dot(source, i, games, layer_weights[...])
    return act, (inner(source, i, games).astype(F32) + jnp.maximum(act, 0.0)).astype(BF16)


def trace_terms(logits_ref, given, games):
    spread = lane_sum(given[8:16], games)
    action = spread[0:1].astype(jnp.int32)
    behave, regul, reward = spread[1:2], spread[2:3], spread[3:4]
    lane = lax.broadcasted_iota(jnp.int32, (1, CH), 1)
    slot = lane % games
    every = logits_ref[...]
    cell_id = lax.broadcasted_iota(jnp.int32, every.shape, 0) * SIDE + lax.broadcasted_iota(
        jnp.int32, every.shape, 1
    )
    lane_full = lax.broadcasted_iota(jnp.int32, every.shape, 2)
    policy_full = lane_full < 4 * games
    taken = (lane_full // games) * CELLS + cell_id == action.reshape(1, 1, CH)
    taken = jnp.where(policy_full, jnp.where(taken, 1.0, 0.0), 0.0)
    logits = jnp.where(policy_full, every, 0.0)

    def over_cells(x):
        return jnp.sum(jnp.sum(x, axis=0), axis=0, keepdims=True)

    exps = jnp.where(policy_full, jnp.exp(logits), 0.0)
    log_total = jnp.log(lane_sum(over_cells(exps), games))
    logp = lane_sum(over_cells(taken * logits), games) - log_total
    value_lane = jnp.where((lane >= 4 * games) & (lane < 5 * games), 1.0, 0.0)
    values = jnp.tanh(lane_sum(over_cells(every) * value_lane, games) / CELLS)

    def ahead(x, by):
        return jnp.where(slot + by < games, pltpu.roll(x, CH - by, 1), 0.0)

    length = given[5:6]
    place = slot.astype(F32)
    live = jnp.where(place < length, 1.0, 0.0)
    next_live = jnp.where(place + 1.0 < length, 1.0, 0.0)
    ratio = jnp.minimum(1.0, jnp.exp(logp - behave))
    shaped = reward - ETA * (logp - regul)
    delta = live * ratio * (shaped + ahead(values, 1) * next_live - values)
    correction, slope = live * delta, live * ratio
    by = 1
    while by < games:
        correction = correction + slope * ahead(correction, by)
        slope = slope * ahead(slope, by)
        by *= 2
    targets = values + correction
    policy_term = -live * ratio * (shaped + ahead(targets, 1) * next_live - values)
    value_term = -live * (targets - values)
    value_cell = value_term * (1.0 - values * values) / CELLS * value_lane
    probs = jnp.exp(logits - log_total.reshape(1, 1, CH))
    logits_ref[...] = jnp.where(
        policy_full,
        policy_term.reshape(1, 1, CH) * (taken - probs),
        jnp.broadcast_to(value_cell.reshape(1, 1, CH), logits.shape),
    )


def learner_part(given, torso, grad, weights, scratch, after_half):
    hs, acts, turned, pre, hidden_grad, cells, heads, total = scratch
    games = 16
    size = ROWS * SIDE * games
    role = lax.axis_index("role")
    h0, h1, a0, a1 = hs.at[0], hs.at[1], acts.at[0], acts.at[1]
    heads[...] = spread_heads(given, games, 5)
    mine = own_lane(games)

    def layer_one(step, i):
        act, h = advance(h0, i, games, weights.at[0])
        pre[0, pl.ds(step * size, size)] = act
        set_inner(h1, i, games, h)

    steps(layer_one)

    def layer_two(step, i):
        act, h = advance(h1, i, games, weights.at[1])
        pre[1, pl.ds(step * size, size)] = act
        cells[pl.ds(i, ROWS)] = head_cells(h, heads, mine, games).reshape(ROWS, SIDE, CH)

    steps(layer_two)
    trace_terms(cells, given, games)

    def top(step, i):
        at = pl.ds(step * size, size)
        g = cells[pl.ds(i, ROWS)].reshape(ROWS * SIDE, 1, CH) * mine[None]
        g = g.reshape(size, CH)
        high = g.astype(BF16)
        low = (g - high.astype(F32)).astype(BF16)
        out = jnp.dot(high, heads[...], preferred_element_type=F32)
        out = out + jnp.dot(low, heads[...], preferred_element_type=F32)
        hidden_grad[at] = out
        set_inner(a1, i, games, jnp.where(pre[1, at] > 0, out, 0.0).astype(BF16))

    steps(top)

    @pl.when(role == 0)
    def _():
        turned[...] = jnp.zeros(turned.shape, BF16)

        def block(offset):
            at = TAPS + offset * CH
            return torso[at : at + CH, :].T.astype(BF16)

        pack(turned, block, True)

        def back(step, i):
            at = pl.ds(step * size, size)
            out = hidden_grad[at] + pair_dot(a1, i, games, turned[...])
            set_inner(a0, i, games, jnp.where(pre[0, at] > 0, out, 0.0).astype(BF16))

        steps(back)

    h, a = hs.at[role], acts.at[role]
    right = [a[1 : SIDE + 1, 2 - q : 2 - q + SIDE].reshape(SIDE * SIDE * games, CH) for q in range(3)]
    right = jnp.concatenate(right, axis=1)
    for half, taps in enumerate(((0, 1), (2,))):
        left = [h[p : p + SIDE, 1 : SIDE + 1].reshape(SIDE * SIDE * games, CH) for p in taps]
        found = lax.dot_general(
            jnp.concatenate(left, axis=1),
            right,
            (((0,), (0,)), ((), ())),
            preferred_element_type=F32,
        )
        for n, p in enumerate(taps):
            for q in range(3):
                at = (3 * p + q) * CH
                grad[at : at + CH, :] = found[n * CH : (n + 1) * CH, q * CH : (q + 1) * CH]
        after_half(half)


def learner_scratch():
    padded = (2, SIDE + 2, SIDE + 2, 16, CH)
    return [
        pltpu.VMEM(padded, BF16),
        pltpu.VMEM(padded, BF16),
        pltpu.VMEM((PACKED, 2 * CH), BF16),
        pltpu.VMEM((2, 1600, CH), F32),
        pltpu.VMEM((1600, CH), F32),
        pltpu.VMEM((SIDE, SIDE, CH), F32),
        pltpu.VMEM((CH, CH), BF16),
        pltpu.VMEM((8, CH), F32),
    ]


def actor_part(given, weights, scratch, games, out, start, ready):
    h0, h1, cells, heads = scratch
    heads[...] = spread_heads(given, games, 4)
    cells[...] = jnp.zeros(cells.shape, F32)
    mine = own_lane(games)
    ready(0)

    def layer_one(step, i):
        _, h = advance(h0, i, games, weights.at[0])
        set_inner(h1, i, games, h)

    steps(layer_one)
    ready(1)

    def layer_two(step, i):
        _, h = advance(h1, i, games, weights.at[1])
        found = head_cells(h, heads, mine, games).reshape(ROWS, SIDE, CH)
        for part in range(ROWS):
            cells[pl.ds((i + part) * SIDE, SIDE), :] = found[part]

    steps(layer_two)
    logits = cells[...]
    cell_id = lax.broadcasted_iota(jnp.int32, logits.shape, 0)
    exps = jnp.where(cell_id < CELLS, jnp.exp(logits), 0.0)
    log_total = jnp.log(lane_sum(jnp.sum(exps, axis=0, keepdims=True), games))
    turned = (logits - log_total).T
    for d in range(4):
        out[pl.ds(start, games), d * CELLS : (d + 1) * CELLS] = turned[
            d * games : (d + 1) * games, 0:CELLS
        ]


def actor_scratch(games):
    padded = (SIDE + 2, SIDE + 2, games, CH)
    return [
        pltpu.VMEM(padded, BF16),
        pltpu.VMEM(padded, BF16),
        pltpu.VMEM((CH, CH), F32),
        pltpu.VMEM((CH, CH), BF16),
    ]


def learner_kernel(traj, given, torso, grad, weights, sem, *scratch):
    hs, acts = scratch[:2]
    for layer in range(2):
        clear_rim(hs.at[layer])
        clear_rim(acts.at[layer])
    copy = pltpu.make_async_copy(traj, center(hs.at[0]), sem)
    copy.start()
    weights[...] = jnp.zeros(weights.shape, BF16)
    for layer in range(2):
        pack_layer(weights, torso, layer)
    copy.wait()
    learner_part(given, torso, grad, weights, scratch, lambda half: None)


def learner(traj, given, torso):
    return pl.pallas_call(
        learner_kernel,
        out_shape=jax.ShapeDtypeStruct((TAPS, CH), F32),
        in_specs=[pl.BlockSpec(memory_space=pl.ANY), vmem(), vmem()],
        out_specs=vmem(),
        scratch_shapes=[pltpu.VMEM((2, PACKED, 2 * CH), BF16), pltpu.SemaphoreType.DMA]
        + learner_scratch(),
        compiler_params=pltpu.CompilerParams(vmem_limit_bytes=48 << 20),
    )(traj, given, torso)


def actor_kernel(games, boards, given, torso, out, weights, sem, *scratch):
    h0, h1 = scratch[:2]
    clear_rim(h0)
    clear_rim(h1)
    start = pl.multiple_of(lax.axis_index("role") * games, games)
    copy = pltpu.make_async_copy(boards.at[:, :, pl.ds(start, games)], center(h0), sem)
    copy.start()
    weights[...] = jnp.zeros(weights.shape, BF16)
    for layer in range(2):
        pack_layer(weights, torso, layer)
    copy.wait()
    actor_part(given, weights, scratch, games, out, 0, lambda layer: None)


def actor(boards, given, torso, games):
    return pl.pallas_call(
        functools.partial(actor_kernel, games),
        out_shape=jax.ShapeDtypeStruct((games, 4 * CELLS), F32),
        in_specs=[pl.BlockSpec(memory_space=pl.ANY), vmem(), vmem()],
        out_specs=vmem(),
        scratch_shapes=[pltpu.VMEM((2, PACKED, 2 * CH), BF16), pltpu.SemaphoreType.DMA]
        + actor_scratch(games),
        compiler_params=pltpu.CompilerParams(vmem_limit_bytes=48 << 20),
    )(boards, given, torso)


def step_kernel(games, boards, traj, *refs):
    parts, (torso, moment_one, moment_two, share_out, out), scratch = refs[:7], refs[7:12], refs[12:]
    (weights, full, torso_in, one_in, two_in, grad, plane, quarter, line, norms) = scratch[:10]
    (s1, r1, s2, r2, sn, rn, sz, rz, sp, rp, ss, rs, sc, rc, loads, send_out, recv_out) = scratch[10:27]
    learner_refs, actor_refs = scratch[27:35], scratch[35:39]
    given, part_refs = scratch[39], scratch[40:]
    share = moment_one.shape[0]
    role = lax.axis_index("role")
    dp = lax.axis_index("dp")
    z, spot = dp // 4, dp % 4
    owner = z // 2 == role
    start = pl.multiple_of(role * games, games)

    def send(src, dst, send_sem, recv_sem, to_role, to_dp):
        copy = pltpu.make_async_remote_copy(
            src_ref=src,
            dst_ref=dst,
            send_sem=send_sem,
            recv_sem=recv_sem,
            device_id=(to_role, to_dp),
            device_id_type=MESH,
        )
        return copy

    barrier = pltpu.get_barrier_semaphore()

    def greet(to_role, to_dp):
        pl.semaphore_signal(barrier, inc=1, device_id=(to_role, to_dp), device_id_type=MESH)

    @pl.when(owner)
    def _():
        for k in range(1, 16):
            other = (dp + k) % 16
            greet(other // 8, other)
        for o in range(2):
            greet(role, (2 - 2 * role + o) * 4 + spot)
        greet(1 - role, dp)

    @pl.when(jnp.logical_not(owner))
    def _():
        for k in range(1, 4):
            greet(role, z * 4 + (spot + k) % 4)
            greet(role, ((z + k) % 4) * 4 + spot)
        greet(1 - role, dp)

    hs, acts = learner_refs[:2]
    clear_rim(hs.at[0])
    load_traj = pltpu.make_async_copy(traj, center(hs.at[0]), loads.at[0])
    load_torso = pltpu.make_async_copy(torso, torso_in, loads.at[1])
    load_one = pltpu.make_async_copy(moment_one, one_in, loads.at[2])
    load_two = pltpu.make_async_copy(moment_two, two_in, loads.at[3])
    load_torso.start()
    load_traj.start()
    clear_rim(actor_refs[0])
    load_boards = pltpu.make_async_copy(
        boards.at[:, :, pl.ds(start, games)], center(actor_refs[0]), loads.at[4]
    )
    load_parts = [
        pltpu.make_async_copy(part, ref, loads.at[5 + n])
        for n, (part, ref) in enumerate(zip(parts, part_refs))
    ]
    for load in load_parts:
        load.start()
    load_one.start()
    load_two.start()
    load_boards.start()
    clear_rim(hs.at[1])
    clear_rim(acts.at[0])
    clear_rim(acts.at[1])
    clear_rim(actor_refs[1])
    for load in load_parts:
        load.wait()
    policy_ref, value_ref, length_ref = part_refs[:3]
    given[...] = jnp.zeros(given.shape, F32)
    given[0:4, :] = policy_ref[...].astype(F32)
    given[4:5, :] = value_ref[...].astype(F32)
    given[5:6, :] = jnp.broadcast_to(length_ref[...].astype(F32), (1, CH))
    for n, ref in enumerate(part_refs[3:]):
        given[8 + n : 9 + n, 0:16] = ref[...].astype(F32)
    weights[...] = jnp.zeros(weights.shape, BF16)
    load_torso.wait()
    for layer in range(2):
        pack_layer(weights, torso_in, layer)
    load_traj.wait()

    def rows(index):
        return pl.ds(pl.multiple_of(index * share, 8), share)

    def to_plane(o, k):
        p = (spot + k) % 4
        return send(
            grad.at[rows(4 * o + p)],
            plane.at[o, spot],
            s1.at[o, k - 1],
            r1.at[o, spot],
            role,
            z * 4 + p,
        )

    def from_plane(o, k):
        p = (spot + k) % 4
        return send(
            grad.at[rows(4 * o + p)], plane.at[o, p], s1.at[o, k - 1], r1.at[o, p], role, z * 4 + p
        )

    def after_half(half):
        if half == 0:

            @pl.when(owner)
            def _():
                pl.semaphore_wait(barrier, 18)

            @pl.when(jnp.logical_not(owner))
            def _():
                pl.semaphore_wait(barrier, 7)

        for k in range(1, 4):
            to_plane(half, k).start()

    learner_part(given, torso_in, grad, weights, learner_refs, after_half)
    load_one.wait()
    load_two.wait()
    load_boards.wait()

    def to_owner(o):
        return send(
            quarter.at[o], line.at[z], s2.at[o], r2.at[z], role, (2 * role + o) * 4 + spot
        )

    for o in range(2):
        summed = grad[rows(4 * o + spot)]
        for k in range(1, 4):
            from_plane(o, k).wait_recv()
            summed = summed + plane[o, (spot + k) % 4]
        quarter[o] = summed

        @pl.when(z != 2 * role + o)
        def _():
            to_owner(o).start()

    half = share // 2
    near = (spot + 1 - 2 * (spot % 2), (spot + 2) % 4)
    places = (spot,) + near + (3 - spot,)

    def share_of(o, place, to_role=None):
        group = role if to_role is None else to_role
        return full.at[rows((2 * group + o) * 4 + place)]

    def half_of(o, place, part):
        begin = ((2 * role + o) * 4 + place) * share + part * half
        return full.at[pl.ds(pl.multiple_of(begin, 8), half)]

    def to_near(o, a):
        at = share_of(o, spot)
        return send(at, at, sp.at[o, a], rp.at[o, a], role, z * 4 + near[a])

    def from_near(o, a):
        at = share_of(o, near[a])
        return send(at, at, sp.at[o, a], rp.at[o, a], role, z * 4 + near[a])

    def to_corner(o, a):
        at = half_of(o, near[a], a)
        return send(at, at, sc.at[o, a], rc.at[o, a], role, z * 4 + near[1 - a])

    def from_corner(o, a):
        at = half_of(o, 3 - spot, a)
        return send(at, at, sc.at[o, a], rc.at[o, a], role, z * 4 + near[1 - a])

    def to_sibling(o, n):
        at = share_of(o, places[n])
        return send(at, at, ss.at[o, n], rs.at[o, n], 1 - role, dp)

    def to_norm(k):
        other = (dp + k) % 16
        return send(norms.at[dp], norms.at[dp], sn.at[k - 1], rn.at[dp], other // 8, other)

    def from_norm(k):
        other = (dp + k) % 16
        return send(norms.at[other], norms.at[other], sn.at[k - 1], rn.at[other], other // 8, other)

    def down_line(k):
        return send(
            full.at[rows(dp)],
            full.at[rows(dp)],
            sz.at[k - 1],
            rz.at[z % 2],
            role,
            ((z + k) % 4) * 4 + spot,
        )

    @pl.when(owner)
    def _():
        summed = quarter[z % 2]
        for k in range(1, 4):
            other = (z + k) % 4
            send(
                quarter.at[0], line.at[other], s2.at[0], r2.at[other], role, other * 4 + spot
            ).wait_recv()
            summed = summed + line[other]
        norms[dp] = jnp.sum((summed * summed).reshape(share // 8, 8, CH), axis=0)
        for k in range(1, 16):
            to_norm(k).start()
        for k in range(1, 16):
            from_norm(k).wait_recv()
        square_sum = jnp.sum(jnp.sum(norms[...], axis=0), axis=0, keepdims=True)
        square_sum = jnp.sum(square_sum, axis=1, keepdims=True)
        size = float(torso.shape[0] * torso.shape[1])
        factor = jnp.minimum(1.0, jnp.sqrt(jnp.full((1, 1), size, F32)) / jnp.sqrt(square_sum + NORM_EPS))
        clipped = summed * factor
        one = BETA_ONE * one_in[...] + (1.0 - BETA_ONE) * clipped
        two = BETA_TWO * two_in[...] + (1.0 - BETA_TWO) * clipped * clipped
        full[rows(dp)] = torso_in[rows(dp)] - LEARN_RATE * one / (jnp.sqrt(two) + ADAM_EPS)
        for k in range(1, 4):
            down_line(k).start()
        for a in range(2):
            to_near(z % 2, a).start()
        to_sibling(z % 2, 0).start()

    same = 1 - (z // 2 + role - 2 * (z // 2) * role)
    first = same * (z % 2) + (1 - same) * (1 - role)
    for o in (first, 1 - first):

        @pl.when(z != 2 * role + o)
        def _():
            at = share_of(o, spot)
            send(at, at, sz.at[0], rz.at[o], role, (2 * role + o) * 4 + spot).wait_recv()
            for a in range(2):
                to_near(o, a).start()
            to_sibling(o, 0).start()

    for o in (first, 1 - first):
        for a in range(2):
            from_near(o, a).wait_recv()
            to_corner(o, a).start()
            to_sibling(o, 1 + a).start()
    for o in (first, 1 - first):
        for a in range(2):
            from_corner(o, a).wait_recv()
        to_sibling(o, 3).start()

    def from_sibling():
        for o in range(2):
            for n in range(4):
                at = share_of(o, places[n], 1 - role)
                send(at, at, ss.at[o, n], rs.at[o, n], 1 - role, dp).wait_recv()

    def ready(layer):
        @pl.when(role == 1 - layer)
        def _():
            from_sibling()

        pack_layer(weights, full, layer)

    actor_part(given, weights, actor_refs, games, out, start, ready)
    share_out[...] = full[rows(dp)]
    mine = out.at[pl.ds(start, games)]
    send(mine, mine, send_out, recv_out, 1 - role, dp).start()
    theirs = out.at[pl.ds(pl.multiple_of((1 - role) * games, games), games)]
    send(mine, theirs, send_out, recv_out, 1 - role, dp).wait_recv()
    send(mine, mine, send_out, recv_out, 1 - role, dp).wait_send()
    for o in range(2):
        for k in range(1, 4):
            to_plane(o, k).wait_send()
        for a in range(2):
            to_near(o, a).wait_send()
            to_corner(o, a).wait_send()
        for k in range(4):
            to_sibling(o, k).wait_send()

        @pl.when(z != 2 * role + o)
        def _():
            to_owner(o).wait_send()

    @pl.when(owner)
    def _():
        for k in range(1, 16):
            to_norm(k).wait_send()
        for k in range(1, 4):
            down_line(k).wait_send()


def step_call(boards, traj, parts, torso, moment_one, moment_two):
    share, games = moment_one.shape[0], boards.shape[2] // 2
    dma = pltpu.SemaphoreType.DMA
    return pl.pallas_call(
        functools.partial(step_kernel, games),
        out_shape=(
            jax.ShapeDtypeStruct((share, CH), F32),
            jax.ShapeDtypeStruct((2 * games, 4 * CELLS), F32),
        ),
        in_specs=[pl.BlockSpec(memory_space=pl.ANY) for _ in range(12)],
        out_specs=(vmem(), vmem()),
        scratch_shapes=[
            pltpu.VMEM((2, PACKED, 2 * CH), BF16),
            pltpu.VMEM((2 * TAPS, CH), F32),
            pltpu.VMEM((2 * TAPS, CH), F32),
            pltpu.VMEM((share, CH), F32),
            pltpu.VMEM((share, CH), F32),
            pltpu.VMEM((TAPS, CH), F32),
            pltpu.VMEM((2, 4, share, CH), F32),
            pltpu.VMEM((2, share, CH), F32),
            pltpu.VMEM((4, share, CH), F32),
            pltpu.VMEM((16, 8, CH), F32),
            dma((2, 3)),
            dma((2, 4)),
            dma((2,)),
            dma((4,)),
            dma((15,)),
            dma((16,)),
            dma((3,)),
            dma((2,)),
            dma((2, 2)),
            dma((2, 2)),
            dma((2, 4)),
            dma((2, 4)),
            dma((2, 2)),
            dma((2, 2)),
            dma((12,)),
            dma,
            dma,
        ]
        + learner_scratch()
        + actor_scratch(games)
        + [pltpu.VMEM((16, CH), F32)]
        + [pltpu.VMEM(part.shape, part.dtype) for part in parts],
        compiler_params=pltpu.CompilerParams(
            collective_id=0, has_side_effects=True, vmem_limit_bytes=56 << 20
        ),
    )(boards, traj, *parts, torso, moment_one, moment_two)


def finish_kernel(share, logp, share_out, logp_out, sems):
    copies = [
        pltpu.make_async_copy(share, share_out, sems.at[0]),
        pltpu.make_async_copy(logp, logp_out, sems.at[1]),
    ]
    for copy in copies:
        copy.start()
    for copy in copies:
        copy.wait()


def finish(share, logp):
    where = pl.BlockSpec(memory_space=pl.ANY)
    return pl.pallas_call(
        finish_kernel,
        out_shape=(
            jax.ShapeDtypeStruct(share.shape, F32),
            jax.ShapeDtypeStruct(logp.shape, F32),
        ),
        in_specs=[where, where],
        out_specs=(where, where),
        scratch_shapes=[pltpu.SemaphoreType.DMA((2,))],
        compiler_params=pltpu.CompilerParams(vmem_limit_bytes=60 << 20),
    )(share, logp)


def update_any(grad, torso, moment_one, moment_two):
    share = moment_one.shape[0]
    summed = lax.all_gather(lax.psum(grad, "dp"), "role", axis=0, tiled=True)
    start = lax.axis_index("dp") * share
    square_sum = jnp.sum(summed * summed)
    factor = jnp.minimum(1.0, jnp.sqrt(float(summed.size)) / jnp.sqrt(square_sum + NORM_EPS))
    clipped = lax.dynamic_slice_in_dim(summed, start, share, 0) * factor
    one = BETA_ONE * moment_one + (1.0 - BETA_ONE) * clipped
    two = BETA_TWO * moment_two + (1.0 - BETA_TWO) * clipped * clipped
    old = lax.dynamic_slice_in_dim(torso, start, share, 0)
    new = old - LEARN_RATE * one / (jnp.sqrt(two) + ADAM_EPS)
    return lax.all_gather(new, "dp", axis=0, tiled=True)


def join_kernel(part, out, send_sem, recv_sem):
    games = part.shape[0]
    role = lax.axis_index("role")
    dp = lax.axis_index("dp")
    barrier = pltpu.get_barrier_semaphore()
    pl.semaphore_signal(barrier, inc=1, device_id=(1 - role, dp), device_id_type=MESH)
    pl.semaphore_wait(barrier, 1)
    mine = pl.ds(pl.multiple_of(role * games, 8), games)
    copy = pltpu.make_async_remote_copy(
        src_ref=part,
        dst_ref=out.at[mine],
        send_sem=send_sem,
        recv_sem=recv_sem,
        device_id=(1 - role, dp),
        device_id_type=MESH,
    )
    copy.start()
    out[mine] = part[...]
    copy.wait()


def join(part):
    return pl.pallas_call(
        join_kernel,
        out_shape=jax.ShapeDtypeStruct((2 * part.shape[0], part.shape[1]), F32),
        in_specs=[vmem()],
        out_specs=vmem(),
        scratch_shapes=[pltpu.SemaphoreType.DMA, pltpu.SemaphoreType.DMA],
        compiler_params=pltpu.CompilerParams(collective_id=1, has_side_effects=True),
    )(part)


def body(
    board_now,
    traj_boards,
    actions,
    lengths,
    behaviour,
    regular,
    rewards,
    torso,
    policy_head,
    value_head,
    first_moment,
    second_moment,
):
    boards = jnp.transpose(board_now, (1, 2, 0, 3))
    traj = jnp.transpose(traj_boards[0], (1, 2, 0, 3))
    if lax.axis_size("dp") == 16 and lax.axis_size("role") == 2:
        parts = (policy_head.T, value_head[None, :], lengths[:, None])
        parts = parts + (actions, behaviour, regular, rewards)
        return finish(*step_call(boards, traj, parts, torso, first_moment, second_moment))

    def wide(x):
        return jnp.pad(x.astype(F32), ((0, 0), (0, CH - x.shape[1])))

    given = jnp.concatenate(
        [
            policy_head.T.astype(F32),
            value_head[None, :].astype(F32),
            jnp.broadcast_to(lengths.astype(F32)[:, None], (1, CH)),
            jnp.zeros((2, CH), F32),
            wide(actions),
            wide(behaviour),
            wide(regular),
            wide(rewards),
            jnp.zeros((4, CH), F32),
        ],
        axis=0,
    )
    grad = learner(traj, given, torso)
    weights = update_any(grad, torso, first_moment, second_moment)
    share_rows = first_moment.shape[0]
    start = lax.axis_index("dp") * share_rows
    new_share = lax.dynamic_slice_in_dim(weights, start, share_rows, 0)
    part = actor(boards, given, weights, board_now.shape[0] // 2)
    return (new_share, join(part))


def solution(mesh):
    return jax.shard_map(
        body,
        mesh=mesh,
        in_specs=(
            P("dp", None, None, None),
            P("dp", None, None, None, None),
            P("dp", None),
            P("dp"),
            P("dp", None),
            P("dp", None),
            P("dp", None),
            P(),
            P(),
            P(),
            P("dp", None),
            P("dp", None),
        ),
        out_specs=(P("dp", None), P("dp", None)),
        check_vma=False,
    )
```

```python
import functools

import jax
import jax.numpy as jnp
from jax import lax
from jax.experimental import pallas as pl
from jax.experimental.pallas import tpu as pltpu
from jax.sharding import PartitionSpec as P

ETA = 0.2
LEARN_RATE = 0.03
BETA_ONE = 0.9
BETA_TWO = 0.999
ADAM_EPS = 1e-08
NORM_EPS = 1e-12
SIDE = 10
CELLS = 100
CH = 128
TAPS = 9 * CH
PACKED = 12 * CH
ROWS = 5
F32 = jnp.float32
BF16 = jnp.bfloat16
MESH = pl.DeviceIdType.MESH


def vmem():
    return pl.BlockSpec(memory_space=pltpu.VMEM)


def pair_columns(padded, i, games):
    parts = []
    for p in range(3):
        for u in range(4):
            cells = [
                padded[pl.ds(i + p, ROWS), u + 2 * m : u + 2 * m + 1] for m in range(SIDE // 2)
            ]
            parts.append(jnp.concatenate(cells, axis=1).reshape(ROWS * SIDE // 2 * games, CH))
    return jnp.concatenate(parts, axis=1)


def pair_dot(padded, i, games, packed):
    both = jnp.dot(pair_columns(padded, i, games), packed, preferred_element_type=F32)
    shape = (ROWS, SIDE // 2, 1, games, CH)
    halves = [both[:, 0:CH].reshape(shape), both[:, CH : 2 * CH].reshape(shape)]
    return jnp.concatenate(halves, axis=2).reshape(ROWS * SIDE * games, CH)


def pack(packed, blocks, back=False):
    for offset in range(9):
        p, q = offset // 3, offset % 3
        block = blocks(offset)
        for cell in range(2):
            row, u = (2 - p, cell + 2 - q) if back else (p, q + cell)
            at = (row * 4 + u) * CH
            packed[at : at + CH, cell * CH : (cell + 1) * CH] = block


def pack_layer(weights, torso, layer):
    def block(offset):
        at = layer * TAPS + offset * CH
        return torso[at : at + CH, :].astype(BF16)

    pack(weights.at[layer], block)


def inner(padded, i, games):
    return padded[pl.ds(i + 1, ROWS), 1 : 1 + SIDE].reshape(ROWS * SIDE * games, CH)


def set_inner(padded, i, games, value):
    padded[pl.ds(i + 1, ROWS), 1 : 1 + SIDE] = value.reshape(ROWS, SIDE, games, CH)


def clear_rim(padded):
    zero = jnp.zeros((1, SIDE + 2) + padded.shape[2:], padded.dtype)
    side = jnp.zeros((SIDE, 1) + padded.shape[2:], padded.dtype)
    padded[0:1] = zero
    padded[SIDE + 1 : SIDE + 2] = zero
    padded[1 : SIDE + 1, 0:1] = side
    padded[1 : SIDE + 1, SIDE + 1 : SIDE + 2] = side


def center(padded):
    return padded.at[pl.ds(1, SIDE), pl.ds(1, SIDE)]


def steps(f):
    for step in range(SIDE // ROWS):
        f(step, step * ROWS)


def lane_sum(x, games):
    shift = 64
    while shift >= games:
        x = x + pltpu.roll(x, shift, 1)
        shift //= 2
    return x


def spread_heads(given, games, amount):
    rows = [jnp.broadcast_to(given[d : d + 1, :], (games, CH)) for d in range(amount)]
    if games * amount < CH:
        rows.append(jnp.zeros((CH - games * amount, CH), F32))
    return jnp.concatenate(rows, axis=0).astype(BF16)


def own_lane(games):
    game = lax.broadcasted_iota(jnp.int32, (games, CH), 0)
    lane = lax.broadcasted_iota(jnp.int32, (games, CH), 1)
    return (lane % games == game).astype(F32)


def head_cells(h, heads, mine, games):
    out = lax.dot_general(h, heads[...], (((1,), (1,)), ((), ())), preferred_element_type=F32)
    return jnp.sum(out.reshape(ROWS * SIDE, games, CH) * mine[None], axis=1)


def advance(source, i, games, layer_weights):
    act = pair_dot(source, i, games, layer_weights[...])
    return act, (inner(source, i, games).astype(F32) + jnp.maximum(act, 0.0)).astype(BF16)


def trace_terms(logits_ref, given, games):
    spread = lane_sum(given[8:16], games)
    action = spread[0:1].astype(jnp.int32)
    behave, regul, reward = spread[1:2], spread[2:3], spread[3:4]
    lane = lax.broadcasted_iota(jnp.int32, (1, CH), 1)
    slot = lane % games
    every = logits_ref[...]
    cell_id = lax.broadcasted_iota(jnp.int32, every.shape, 0) * SIDE + lax.broadcasted_iota(
        jnp.int32, every.shape, 1
    )
    lane_full = lax.broadcasted_iota(jnp.int32, every.shape, 2)
    policy_full = lane_full < 4 * games
    taken = (lane_full // games) * CELLS + cell_id == action.reshape(1, 1, CH)
    taken = jnp.where(policy_full, jnp.where(taken, 1.0, 0.0), 0.0)
    logits = jnp.where(policy_full, every, 0.0)

    def over_cells(x):
        return jnp.sum(jnp.sum(x, axis=0), axis=0, keepdims=True)

    exps = jnp.where(policy_full, jnp.exp(logits), 0.0)
    log_total = jnp.log(lane_sum(over_cells(exps), games))
    logp = lane_sum(over_cells(taken * logits), games) - log_total
    value_lane = jnp.where((lane >= 4 * games) & (lane < 5 * games), 1.0, 0.0)
    values = jnp.tanh(lane_sum(over_cells(every) * value_lane, games) / CELLS)

    def ahead(x, by):
        return jnp.where(slot + by < games, pltpu.roll(x, CH - by, 1), 0.0)

    length = given[5:6]
    place = slot.astype(F32)
    live = jnp.where(place < length, 1.0, 0.0)
    next_live = jnp.where(place + 1.0 < length, 1.0, 0.0)
    ratio = jnp.minimum(1.0, jnp.exp(logp - behave))
    shaped = reward - ETA * (logp - regul)
    delta = live * ratio * (shaped + ahead(values, 1) * next_live - values)
    correction, slope = live * delta, live * ratio
    by = 1
    while by < games:
        correction = correction + slope * ahead(correction, by)
        slope = slope * ahead(slope, by)
        by *= 2
    targets = values + correction
    policy_term = -live * ratio * (shaped + ahead(targets, 1) * next_live - values)
    value_term = -live * (targets - values)
    value_cell = value_term * (1.0 - values * values) / CELLS * value_lane
    probs = jnp.exp(logits - log_total.reshape(1, 1, CH))
    logits_ref[...] = jnp.where(
        policy_full,
        policy_term.reshape(1, 1, CH) * (taken - probs),
        jnp.broadcast_to(value_cell.reshape(1, 1, CH), logits.shape),
    )


def learner_part(given, torso, grad, weights, scratch, after_half):
    hs, acts, turned, pre, hidden_grad, cells, heads, total = scratch
    games = 16
    size = ROWS * SIDE * games
    role = lax.axis_index("role")
    h0, h1, a0, a1 = hs.at[0], hs.at[1], acts.at[0], acts.at[1]
    heads[...] = spread_heads(given, games, 5)
    mine = own_lane(games)

    def layer_one(step, i):
        act, h = advance(h0, i, games, weights.at[0])
        pre[0, pl.ds(step * size, size)] = act
        set_inner(h1, i, games, h)

    steps(layer_one)

    def layer_two(step, i):
        act, h = advance(h1, i, games, weights.at[1])
        pre[1, pl.ds(step * size, size)] = act
        cells[pl.ds(i, ROWS)] = head_cells(h, heads, mine, games).reshape(ROWS, SIDE, CH)

    steps(layer_two)
    trace_terms(cells, given, games)

    def top(step, i):
        at = pl.ds(step * size, size)
        g = cells[pl.ds(i, ROWS)].reshape(ROWS * SIDE, 1, CH) * mine[None]
        g = g.reshape(size, CH)
        high = g.astype(BF16)
        low = (g - high.astype(F32)).astype(BF16)
        out = jnp.dot(high, heads[...], preferred_element_type=F32)
        out = out + jnp.dot(low, heads[...], preferred_element_type=F32)
        hidden_grad[at] = out
        set_inner(a1, i, games, jnp.where(pre[1, at] > 0, out, 0.0).astype(BF16))

    steps(top)

    @pl.when(role == 0)
    def _():
        turned[...] = jnp.zeros(turned.shape, BF16)

        def block(offset):
            at = TAPS + offset * CH
            return torso[at : at + CH, :].T.astype(BF16)

        pack(turned, block, True)

        def back(step, i):
            at = pl.ds(step * size, size)
            out = hidden_grad[at] + pair_dot(a1, i, games, turned[...])
            set_inner(a0, i, games, jnp.where(pre[0, at] > 0, out, 0.0).astype(BF16))

        steps(back)

    h, a = hs.at[role], acts.at[role]
    right = [a[1 : SIDE + 1, 2 - q : 2 - q + SIDE].reshape(SIDE * SIDE * games, CH) for q in range(3)]
    right = jnp.concatenate(right, axis=1)
    for half, taps in enumerate(((0, 1), (2,))):
        left = [h[p : p + SIDE, 1 : SIDE + 1].reshape(SIDE * SIDE * games, CH) for p in taps]
        found = lax.dot_general(
            jnp.concatenate(left, axis=1),
            right,
            (((0,), (0,)), ((), ())),
            preferred_element_type=F32,
        )
        for n, p in enumerate(taps):
            for q in range(3):
                at = (3 * p + q) * CH
                grad[at : at + CH, :] = found[n * CH : (n + 1) * CH, q * CH : (q + 1) * CH]
        after_half(half)


def learner_scratch():
    padded = (2, SIDE + 2, SIDE + 2, 16, CH)
    return [
        pltpu.VMEM(padded, BF16),
        pltpu.VMEM(padded, BF16),
        pltpu.VMEM((PACKED, 2 * CH), BF16),
        pltpu.VMEM((2, 1600, CH), F32),
        pltpu.VMEM((1600, CH), F32),
        pltpu.VMEM((SIDE, SIDE, CH), F32),
        pltpu.VMEM((CH, CH), BF16),
        pltpu.VMEM((8, CH), F32),
    ]


def actor_part(given, weights, scratch, games, out, start, ready):
    h0, h1, cells, heads = scratch
    heads[...] = spread_heads(given, games, 4)
    cells[...] = jnp.zeros(cells.shape, F32)
    mine = own_lane(games)
    ready(0)

    def layer_one(step, i):
        _, h = advance(h0, i, games, weights.at[0])
        set_inner(h1, i, games, h)

    steps(layer_one)
    ready(1)

    def layer_two(step, i):
        _, h = advance(h1, i, games, weights.at[1])
        found = head_cells(h, heads, mine, games).reshape(ROWS, SIDE, CH)
        for part in range(ROWS):
            cells[pl.ds((i + part) * SIDE, SIDE), :] = found[part]

    steps(layer_two)
    logits = cells[...]
    cell_id = lax.broadcasted_iota(jnp.int32, logits.shape, 0)
    exps = jnp.where(cell_id < CELLS, jnp.exp(logits), 0.0)
    log_total = jnp.log(lane_sum(jnp.sum(exps, axis=0, keepdims=True), games))
    turned = (logits - log_total).T
    for d in range(4):
        out[pl.ds(start, games), d * CELLS : (d + 1) * CELLS] = turned[
            d * games : (d + 1) * games, 0:CELLS
        ]


def actor_scratch(games):
    padded = (SIDE + 2, SIDE + 2, games, CH)
    return [
        pltpu.VMEM(padded, BF16),
        pltpu.VMEM(padded, BF16),
        pltpu.VMEM((CH, CH), F32),
        pltpu.VMEM((CH, CH), BF16),
    ]


def learner_kernel(traj, given, torso, grad, weights, sem, *scratch):
    hs, acts = scratch[:2]
    for layer in range(2):
        clear_rim(hs.at[layer])
        clear_rim(acts.at[layer])
    copy = pltpu.make_async_copy(traj, center(hs.at[0]), sem)
    copy.start()
    weights[...] = jnp.zeros(weights.shape, BF16)
    for layer in range(2):
        pack_layer(weights, torso, layer)
    copy.wait()
    learner_part(given, torso, grad, weights, scratch, lambda half: None)


def learner(traj, given, torso):
    return pl.pallas_call(
        learner_kernel,
        out_shape=jax.ShapeDtypeStruct((TAPS, CH), F32),
        in_specs=[pl.BlockSpec(memory_space=pl.ANY), vmem(), vmem()],
        out_specs=vmem(),
        scratch_shapes=[pltpu.VMEM((2, PACKED, 2 * CH), BF16), pltpu.SemaphoreType.DMA]
        + learner_scratch(),
        compiler_params=pltpu.CompilerParams(vmem_limit_bytes=48 << 20),
    )(traj, given, torso)


def actor_kernel(games, boards, given, torso, out, weights, sem, *scratch):
    h0, h1 = scratch[:2]
    clear_rim(h0)
    clear_rim(h1)
    start = pl.multiple_of(lax.axis_index("role") * games, games)
    copy = pltpu.make_async_copy(boards.at[:, :, pl.ds(start, games)], center(h0), sem)
    copy.start()
    weights[...] = jnp.zeros(weights.shape, BF16)
    for layer in range(2):
        pack_layer(weights, torso, layer)
    copy.wait()
    actor_part(given, weights, scratch, games, out, 0, lambda layer: None)


def actor(boards, given, torso, games):
    return pl.pallas_call(
        functools.partial(actor_kernel, games),
        out_shape=jax.ShapeDtypeStruct((games, 4 * CELLS), F32),
        in_specs=[pl.BlockSpec(memory_space=pl.ANY), vmem(), vmem()],
        out_specs=vmem(),
        scratch_shapes=[pltpu.VMEM((2, PACKED, 2 * CH), BF16), pltpu.SemaphoreType.DMA]
        + actor_scratch(games),
        compiler_params=pltpu.CompilerParams(vmem_limit_bytes=48 << 20),
    )(boards, given, torso)


def step_kernel(games, boards, traj, *refs):
    parts, (torso, moment_one, moment_two, share_out, out), scratch = refs[:7], refs[7:12], refs[12:]
    (weights, full, torso_in, one_in, two_in, grad, plane, quarter, line, norms) = scratch[:10]
    (s1, r1, s2, r2, sn, rn, sz, rz, sp, rp, ss, rs, loads, send_out, recv_out) = scratch[10:25]
    learner_refs, actor_refs = scratch[25:33], scratch[33:37]
    given, part_refs = scratch[37], scratch[38:]
    share = moment_one.shape[0]
    role = lax.axis_index("role")
    dp = lax.axis_index("dp")
    z, spot = dp // 4, dp % 4
    owner = z // 2 == role
    start = pl.multiple_of(role * games, games)

    def send(src, dst, send_sem, recv_sem, to_role, to_dp):
        copy = pltpu.make_async_remote_copy(
            src_ref=src,
            dst_ref=dst,
            send_sem=send_sem,
            recv_sem=recv_sem,
            device_id=(to_role, to_dp),
            device_id_type=MESH,
        )
        return copy

    barrier = pltpu.get_barrier_semaphore()

    def greet(to_role, to_dp):
        pl.semaphore_signal(barrier, inc=1, device_id=(to_role, to_dp), device_id_type=MESH)

    @pl.when(owner)
    def _():
        for k in range(1, 16):
            other = (dp + k) % 16
            greet(other // 8, other)
        for o in range(2):
            greet(role, (2 - 2 * role + o) * 4 + spot)
        greet(1 - role, dp)

    @pl.when(jnp.logical_not(owner))
    def _():
        for k in range(1, 4):
            greet(role, z * 4 + (spot + k) % 4)
            greet(role, ((z + k) % 4) * 4 + spot)
        greet(1 - role, dp)

    hs, acts = learner_refs[:2]
    clear_rim(hs.at[0])
    load_traj = pltpu.make_async_copy(traj, center(hs.at[0]), loads.at[0])
    load_torso = pltpu.make_async_copy(torso, torso_in, loads.at[1])
    load_one = pltpu.make_async_copy(moment_one, one_in, loads.at[2])
    load_two = pltpu.make_async_copy(moment_two, two_in, loads.at[3])
    load_torso.start()
    load_traj.start()
    clear_rim(actor_refs[0])
    load_boards = pltpu.make_async_copy(
        boards.at[:, :, pl.ds(start, games)], center(actor_refs[0]), loads.at[4]
    )
    load_parts = [
        pltpu.make_async_copy(part, ref, loads.at[5 + n])
        for n, (part, ref) in enumerate(zip(parts, part_refs))
    ]
    for load in load_parts:
        load.start()
    load_one.start()
    load_two.start()
    load_boards.start()
    clear_rim(hs.at[1])
    clear_rim(acts.at[0])
    clear_rim(acts.at[1])
    clear_rim(actor_refs[1])
    for load in load_parts:
        load.wait()
    policy_ref, value_ref, length_ref = part_refs[:3]
    given[...] = jnp.zeros(given.shape, F32)
    given[0:4, :] = policy_ref[...].astype(F32)
    given[4:5, :] = value_ref[...].astype(F32)
    given[5:6, :] = jnp.broadcast_to(length_ref[...].astype(F32), (1, CH))
    for n, ref in enumerate(part_refs[3:]):
        given[8 + n : 9 + n, 0:16] = ref[...].astype(F32)
    weights[...] = jnp.zeros(weights.shape, BF16)
    load_torso.wait()
    for layer in range(2):
        pack_layer(weights, torso_in, layer)
    load_traj.wait()

    def rows(index):
        return pl.ds(pl.multiple_of(index * share, 8), share)

    def to_plane(o, k):
        p = (spot + k) % 4
        return send(
            grad.at[rows(4 * o + p)],
            plane.at[o, spot],
            s1.at[o, k - 1],
            r1.at[o, spot],
            role,
            z * 4 + p,
        )

    def from_plane(o, k):
        p = (spot + k) % 4
        return send(
            grad.at[rows(4 * o + p)], plane.at[o, p], s1.at[o, k - 1], r1.at[o, p], role, z * 4 + p
        )

    def after_half(half):
        if half == 0:

            @pl.when(owner)
            def _():
                pl.semaphore_wait(barrier, 18)

            @pl.when(jnp.logical_not(owner))
            def _():
                pl.semaphore_wait(barrier, 7)

        for k in range(1, 4):
            to_plane(half, k).start()

    learner_part(given, torso_in, grad, weights, learner_refs, after_half)
    load_one.wait()
    load_two.wait()
    load_boards.wait()

    def to_owner(o):
        return send(
            quarter.at[o], line.at[z], s2.at[o], r2.at[z], role, (2 * role + o) * 4 + spot
        )

    for o in range(2):
        summed = grad[rows(4 * o + spot)]
        for k in range(1, 4):
            from_plane(o, k).wait_recv()
            summed = summed + plane[o, (spot + k) % 4]
        quarter[o] = summed

        @pl.when(z != 2 * role + o)
        def _():
            to_owner(o).start()

    others = tuple((spot + k) % 4 for k in range(1, 4))
    places = (spot,) + others

    def share_of(o, place, to_role=None):
        group = role if to_role is None else to_role
        return full.at[rows((2 * group + o) * 4 + place)]

    def to_near(o, a):
        at = share_of(o, spot)
        return send(at, at, sp.at[o, a], rp.at[o, 2 - a], role, z * 4 + others[a])

    def from_near(o, a):
        at = share_of(o, others[a])
        return send(at, at, sp.at[o, a], rp.at[o, a], role, z * 4 + others[a])

    def to_sibling(o, n):
        at = share_of(o, places[n])
        return send(at, at, ss.at[o, n], rs.at[o, n], 1 - role, dp)

    def to_norm(k):
        other = (dp + k) % 16
        return send(norms.at[dp], norms.at[dp], sn.at[k - 1], rn.at[dp], other // 8, other)

    def from_norm(k):
        other = (dp + k) % 16
        return send(norms.at[other], norms.at[other], sn.at[k - 1], rn.at[other], other // 8, other)

    def down_line(k):
        return send(
            full.at[rows(dp)],
            full.at[rows(dp)],
            sz.at[k - 1],
            rz.at[z % 2],
            role,
            ((z + k) % 4) * 4 + spot,
        )

    @pl.when(owner)
    def _():
        summed = quarter[z % 2]
        for k in range(1, 4):
            other = (z + k) % 4
            send(
                quarter.at[0], line.at[other], s2.at[0], r2.at[other], role, other * 4 + spot
            ).wait_recv()
            summed = summed + line[other]
        norms[dp] = jnp.sum((summed * summed).reshape(share // 8, 8, CH), axis=0)
        for k in range(1, 16):
            to_norm(k).start()
        for k in range(1, 16):
            from_norm(k).wait_recv()
        square_sum = jnp.sum(jnp.sum(norms[...], axis=0), axis=0, keepdims=True)
        square_sum = jnp.sum(square_sum, axis=1, keepdims=True)
        size = float(torso.shape[0] * torso.shape[1])
        factor = jnp.minimum(1.0, jnp.sqrt(jnp.full((1, 1), size, F32)) / jnp.sqrt(square_sum + NORM_EPS))
        clipped = summed * factor
        one = BETA_ONE * one_in[...] + (1.0 - BETA_ONE) * clipped
        two = BETA_TWO * two_in[...] + (1.0 - BETA_TWO) * clipped * clipped
        full[rows(dp)] = torso_in[rows(dp)] - LEARN_RATE * one / (jnp.sqrt(two) + ADAM_EPS)
        for k in range(1, 4):
            down_line(k).start()
        for a in range(3):
            to_near(z % 2, a).start()
        to_sibling(z % 2, 0).start()

    same = 1 - (z // 2 + role - 2 * (z // 2) * role)
    first = same * (z % 2) + (1 - same) * (1 - role)
    for o in (first, 1 - first):

        @pl.when(z != 2 * role + o)
        def _():
            at = share_of(o, spot)
            send(at, at, sz.at[0], rz.at[o], role, (2 * role + o) * 4 + spot).wait_recv()
            for a in range(3):
                to_near(o, a).start()
            to_sibling(o, 0).start()

    for o in (first, 1 - first):
        for a in range(3):
            from_near(o, a).wait_recv()
            to_sibling(o, 1 + a).start()

    for o in range(2):
        for k in range(1, 4):
            to_plane(o, k).wait_send()

        @pl.when(z != 2 * role + o)
        def _():
            to_owner(o).wait_send()

    @pl.when(owner)
    def _():
        for k in range(1, 16):
            to_norm(k).wait_send()
        for k in range(1, 4):
            down_line(k).wait_send()

    def from_sibling():
        for o in range(2):
            for n in range(4):
                at = share_of(o, places[n], 1 - role)
                send(at, at, ss.at[o, n], rs.at[o, n], 1 - role, dp).wait_recv()

    def ready(layer):
        @pl.when(role == 1 - layer)
        def _():
            from_sibling()

        pack_layer(weights, full, layer)

    actor_part(given, weights, actor_refs, games, out, start, ready)
    mine = out.at[pl.ds(start, games)]
    send(mine, mine, send_out, recv_out, 1 - role, dp).start()
    share_out[...] = full[rows(dp)]
    for o in range(2):
        for a in range(3):
            to_near(o, a).wait_send()
        for n in range(4):
            to_sibling(o, n).wait_send()
    theirs = out.at[pl.ds(pl.multiple_of((1 - role) * games, games), games)]
    send(mine, theirs, send_out, recv_out, 1 - role, dp).wait_recv()
    send(mine, mine, send_out, recv_out, 1 - role, dp).wait_send()


def step_call(boards, traj, parts, torso, moment_one, moment_two):
    share, games = moment_one.shape[0], boards.shape[2] // 2
    dma = pltpu.SemaphoreType.DMA
    return pl.pallas_call(
        functools.partial(step_kernel, games),
        out_shape=(
            jax.ShapeDtypeStruct((share, CH), F32),
            jax.ShapeDtypeStruct((2 * games, 4 * CELLS), F32),
        ),
        in_specs=[pl.BlockSpec(memory_space=pl.ANY) for _ in range(12)],
        out_specs=(vmem(), vmem()),
        scratch_shapes=[
            pltpu.VMEM((2, PACKED, 2 * CH), BF16),
            pltpu.VMEM((2 * TAPS, CH), F32),
            pltpu.VMEM((2 * TAPS, CH), F32),
            pltpu.VMEM((share, CH), F32),
            pltpu.VMEM((share, CH), F32),
            pltpu.VMEM((TAPS, CH), F32),
            pltpu.VMEM((2, 4, share, CH), F32),
            pltpu.VMEM((2, share, CH), F32),
            pltpu.VMEM((4, share, CH), F32),
            pltpu.VMEM((16, 8, CH), F32),
            dma((2, 3)),
            dma((2, 4)),
            dma((2,)),
            dma((4,)),
            dma((15,)),
            dma((16,)),
            dma((3,)),
            dma((2,)),
            dma((2, 3)),
            dma((2, 3)),
            dma((2, 4)),
            dma((2, 4)),
            dma((12,)),
            dma,
            dma,
        ]
        + learner_scratch()
        + actor_scratch(games)
        + [pltpu.VMEM((16, CH), F32)]
        + [pltpu.VMEM(part.shape, part.dtype) for part in parts],
        compiler_params=pltpu.CompilerParams(
            collective_id=0, has_side_effects=True, vmem_limit_bytes=56 << 20
        ),
    )(boards, traj, *parts, torso, moment_one, moment_two)


def finish_kernel(share, logp, share_out, logp_out, share_at, logp_at, sems):
    reads = [
        pltpu.make_async_copy(share, share_at, sems.at[0]),
        pltpu.make_async_copy(logp, logp_at, sems.at[1]),
    ]
    writes = [
        pltpu.make_async_copy(share_at, share_out, sems.at[2]),
        pltpu.make_async_copy(logp_at, logp_out, sems.at[3]),
    ]
    for read in reads:
        read.start()
    for read, write in zip(reads, writes):
        read.wait()
        write.start()
    for write in writes:
        write.wait()


def finish(share, logp):
    where = pl.BlockSpec(memory_space=pl.ANY)
    return pl.pallas_call(
        finish_kernel,
        out_shape=(
            jax.ShapeDtypeStruct(share.shape, F32),
            jax.ShapeDtypeStruct(logp.shape, F32),
        ),
        in_specs=[where, where],
        out_specs=(where, where),
        scratch_shapes=[
            pltpu.VMEM(share.shape, F32),
            pltpu.VMEM(logp.shape, F32),
            pltpu.SemaphoreType.DMA((4,)),
        ],
        compiler_params=pltpu.CompilerParams(vmem_limit_bytes=60 << 20),
    )(share, logp)


def update_any(grad, torso, moment_one, moment_two):
    share = moment_one.shape[0]
    summed = lax.all_gather(lax.psum(grad, "dp"), "role", axis=0, tiled=True)
    start = lax.axis_index("dp") * share
    square_sum = jnp.sum(summed * summed)
    factor = jnp.minimum(1.0, jnp.sqrt(float(summed.size)) / jnp.sqrt(square_sum + NORM_EPS))
    clipped = lax.dynamic_slice_in_dim(summed, start, share, 0) * factor
    one = BETA_ONE * moment_one + (1.0 - BETA_ONE) * clipped
    two = BETA_TWO * moment_two + (1.0 - BETA_TWO) * clipped * clipped
    old = lax.dynamic_slice_in_dim(torso, start, share, 0)
    new = old - LEARN_RATE * one / (jnp.sqrt(two) + ADAM_EPS)
    return lax.all_gather(new, "dp", axis=0, tiled=True)


def join_kernel(part, out, send_sem, recv_sem):
    games = part.shape[0]
    role = lax.axis_index("role")
    dp = lax.axis_index("dp")
    barrier = pltpu.get_barrier_semaphore()
    pl.semaphore_signal(barrier, inc=1, device_id=(1 - role, dp), device_id_type=MESH)
    pl.semaphore_wait(barrier, 1)
    mine = pl.ds(pl.multiple_of(role * games, 8), games)
    copy = pltpu.make_async_remote_copy(
        src_ref=part,
        dst_ref=out.at[mine],
        send_sem=send_sem,
        recv_sem=recv_sem,
        device_id=(1 - role, dp),
        device_id_type=MESH,
    )
    copy.start()
    out[mine] = part[...]
    copy.wait()


def join(part):
    return pl.pallas_call(
        join_kernel,
        out_shape=jax.ShapeDtypeStruct((2 * part.shape[0], part.shape[1]), F32),
        in_specs=[vmem()],
        out_specs=vmem(),
        scratch_shapes=[pltpu.SemaphoreType.DMA, pltpu.SemaphoreType.DMA],
        compiler_params=pltpu.CompilerParams(collective_id=1, has_side_effects=True),
    )(part)


def body(
    board_now,
    traj_boards,
    actions,
    lengths,
    behaviour,
    regular,
    rewards,
    torso,
    policy_head,
    value_head,
    first_moment,
    second_moment,
):
    boards = jnp.transpose(board_now, (1, 2, 0, 3))
    traj = jnp.transpose(traj_boards[0], (1, 2, 0, 3))
    if lax.axis_size("dp") == 16 and lax.axis_size("role") == 2:
        parts = (policy_head.T, value_head[None, :], lengths[:, None])
        parts = parts + (actions, behaviour, regular, rewards)
        return finish(*step_call(boards, traj, parts, torso, first_moment, second_moment))

    def wide(x):
        return jnp.pad(x.astype(F32), ((0, 0), (0, CH - x.shape[1])))

    given = jnp.concatenate(
        [
            policy_head.T.astype(F32),
            value_head[None, :].astype(F32),
            jnp.broadcast_to(lengths.astype(F32)[:, None], (1, CH)),
            jnp.zeros((2, CH), F32),
            wide(actions),
            wide(behaviour),
            wide(regular),
            wide(rewards),
            jnp.zeros((4, CH), F32),
        ],
        axis=0,
    )
    grad = learner(traj, given, torso)
    weights = update_any(grad, torso, first_moment, second_moment)
    share_rows = first_moment.shape[0]
    start = lax.axis_index("dp") * share_rows
    new_share = lax.dynamic_slice_in_dim(weights, start, share_rows, 0)
    part = actor(boards, given, weights, board_now.shape[0] // 2)
    return (new_share, join(part))


def solution(mesh):
    return jax.shard_map(
        body,
        mesh=mesh,
        in_specs=(
            P("dp", None, None, None),
            P("dp", None, None, None, None),
            P("dp", None),
            P("dp"),
            P("dp", None),
            P("dp", None),
            P("dp", None),
            P(),
            P(),
            P(),
            P("dp", None),
            P("dp", None),
        ),
        out_specs=(P("dp", None), P("dp", None)),
        check_vma=False,
    )
```

```python
import functools

import jax
import jax.numpy as jnp
from jax import lax
from jax.experimental import pallas as pl
from jax.experimental.pallas import tpu as pltpu
from jax.sharding import PartitionSpec as P

ETA = 0.2
LEARN_RATE = 0.03
BETA_ONE = 0.9
BETA_TWO = 0.999
ADAM_EPS = 1e-08
NORM_EPS = 1e-12
SIDE = 10
CELLS = 100
CH = 128
TAPS = 9 * CH
PACKED = 12 * CH
ROWS = 5
F32 = jnp.float32
BF16 = jnp.bfloat16
MESH = pl.DeviceIdType.MESH


def vmem():
    return pl.BlockSpec(memory_space=pltpu.VMEM)


def pair_columns(padded, i, games):
    parts = []
    for p in range(3):
        for u in range(4):
            cells = [
                padded[pl.ds(i + p, ROWS), u + 2 * m : u + 2 * m + 1] for m in range(SIDE // 2)
            ]
            parts.append(jnp.concatenate(cells, axis=1).reshape(ROWS * SIDE // 2 * games, CH))
    return jnp.concatenate(parts, axis=1)


def pair_dot(padded, i, games, packed):
    both = jnp.dot(pair_columns(padded, i, games), packed, preferred_element_type=F32)
    shape = (ROWS, SIDE // 2, 1, games, CH)
    halves = [both[:, 0:CH].reshape(shape), both[:, CH : 2 * CH].reshape(shape)]
    return jnp.concatenate(halves, axis=2).reshape(ROWS * SIDE * games, CH)


def pack(packed, blocks, back=False):
    for offset in range(9):
        p, q = offset // 3, offset % 3
        block = blocks(offset)
        for cell in range(2):
            row, u = (2 - p, cell + 2 - q) if back else (p, q + cell)
            at = (row * 4 + u) * CH
            packed[at : at + CH, cell * CH : (cell + 1) * CH] = block


def pack_layer(weights, torso, layer):
    def block(offset):
        at = layer * TAPS + offset * CH
        return torso[at : at + CH, :].astype(BF16)

    pack(weights.at[layer], block)


def inner(padded, i, games):
    return padded[pl.ds(i + 1, ROWS), 1 : 1 + SIDE].reshape(ROWS * SIDE * games, CH)


def set_inner(padded, i, games, value):
    padded[pl.ds(i + 1, ROWS), 1 : 1 + SIDE] = value.reshape(ROWS, SIDE, games, CH)


def clear_rim(padded):
    zero = jnp.zeros((1, SIDE + 2) + padded.shape[2:], padded.dtype)
    side = jnp.zeros((SIDE, 1) + padded.shape[2:], padded.dtype)
    padded[0:1] = zero
    padded[SIDE + 1 : SIDE + 2] = zero
    padded[1 : SIDE + 1, 0:1] = side
    padded[1 : SIDE + 1, SIDE + 1 : SIDE + 2] = side


def center(padded):
    return padded.at[pl.ds(1, SIDE), pl.ds(1, SIDE)]


def steps(f):
    for step in range(SIDE // ROWS):
        f(step, step * ROWS)


def lane_sum(x, games):
    shift = 64
    while shift >= games:
        x = x + pltpu.roll(x, shift, 1)
        shift //= 2
    return x


def spread_heads(given, games, amount):
    rows = [jnp.broadcast_to(given[d : d + 1, :], (games, CH)) for d in range(amount)]
    if games * amount < CH:
        rows.append(jnp.zeros((CH - games * amount, CH), F32))
    return jnp.concatenate(rows, axis=0).astype(BF16)


def own_lane(games):
    game = lax.broadcasted_iota(jnp.int32, (games, CH), 0)
    lane = lax.broadcasted_iota(jnp.int32, (games, CH), 1)
    return (lane % games == game).astype(F32)


def head_cells(h, heads, mine, games):
    out = lax.dot_general(h, heads[...], (((1,), (1,)), ((), ())), preferred_element_type=F32)
    return jnp.sum(out.reshape(ROWS * SIDE, games, CH) * mine[None], axis=1)


def advance(source, i, games, layer_weights):
    act = pair_dot(source, i, games, layer_weights[...])
    return act, (inner(source, i, games).astype(F32) + jnp.maximum(act, 0.0)).astype(BF16)


def trace_terms(logits_ref, given, games):
    spread = lane_sum(given[8:16], games)
    action = spread[0:1].astype(jnp.int32)
    behave, regul, reward = spread[1:2], spread[2:3], spread[3:4]
    lane = lax.broadcasted_iota(jnp.int32, (1, CH), 1)
    slot = lane % games
    every = logits_ref[...]
    cell_id = lax.broadcasted_iota(jnp.int32, every.shape, 0) * SIDE + lax.broadcasted_iota(
        jnp.int32, every.shape, 1
    )
    lane_full = lax.broadcasted_iota(jnp.int32, every.shape, 2)
    policy_full = lane_full < 4 * games
    taken = (lane_full // games) * CELLS + cell_id == action.reshape(1, 1, CH)
    taken = jnp.where(policy_full, jnp.where(taken, 1.0, 0.0), 0.0)
    logits = jnp.where(policy_full, every, 0.0)

    def over_cells(x):
        return jnp.sum(jnp.sum(x, axis=0), axis=0, keepdims=True)

    exps = jnp.where(policy_full, jnp.exp(logits), 0.0)
    log_total = jnp.log(lane_sum(over_cells(exps), games))
    logp = lane_sum(over_cells(taken * logits), games) - log_total
    value_lane = jnp.where((lane >= 4 * games) & (lane < 5 * games), 1.0, 0.0)
    values = jnp.tanh(lane_sum(over_cells(every) * value_lane, games) / CELLS)

    def ahead(x, by):
        return jnp.where(slot + by < games, pltpu.roll(x, CH - by, 1), 0.0)

    length = given[5:6]
    place = slot.astype(F32)
    live = jnp.where(place < length, 1.0, 0.0)
    next_live = jnp.where(place + 1.0 < length, 1.0, 0.0)
    ratio = jnp.minimum(1.0, jnp.exp(logp - behave))
    shaped = reward - ETA * (logp - regul)
    delta = live * ratio * (shaped + ahead(values, 1) * next_live - values)
    correction, slope = live * delta, live * ratio
    by = 1
    while by < games:
        correction = correction + slope * ahead(correction, by)
        slope = slope * ahead(slope, by)
        by *= 2
    targets = values + correction
    policy_term = -live * ratio * (shaped + ahead(targets, 1) * next_live - values)
    value_term = -live * (targets - values)
    value_cell = value_term * (1.0 - values * values) / CELLS * value_lane
    probs = jnp.exp(logits - log_total.reshape(1, 1, CH))
    logits_ref[...] = jnp.where(
        policy_full,
        policy_term.reshape(1, 1, CH) * (taken - probs),
        jnp.broadcast_to(value_cell.reshape(1, 1, CH), logits.shape),
    )


def learner_part(given, torso, grad, weights, scratch, after_half):
    hs, acts, turned, pre, hidden_grad, cells, heads, total = scratch
    games = 16
    size = ROWS * SIDE * games
    role = lax.axis_index("role")
    h0, h1, a0, a1 = hs.at[0], hs.at[1], acts.at[0], acts.at[1]
    heads[...] = spread_heads(given, games, 5)
    mine = own_lane(games)

    def layer_one(step, i):
        act, h = advance(h0, i, games, weights.at[0])
        pre[0, pl.ds(step * size, size)] = act
        set_inner(h1, i, games, h)

    steps(layer_one)
    pack_layer(weights, torso, 1)
    turned[...] = jnp.zeros(turned.shape, BF16)

    def block(offset):
        at = TAPS + offset * CH
        return torso[at : at + CH, :].T.astype(BF16)

    pack(turned, block, True)

    def layer_two(step, i):
        act, h = advance(h1, i, games, weights.at[1])
        pre[1, pl.ds(step * size, size)] = act
        cells[pl.ds(i, ROWS)] = head_cells(h, heads, mine, games).reshape(ROWS, SIDE, CH)

    steps(layer_two)
    trace_terms(cells, given, games)

    def top(step, i):
        at = pl.ds(step * size, size)
        g = cells[pl.ds(i, ROWS)].reshape(ROWS * SIDE, 1, CH) * mine[None]
        g = g.reshape(size, CH)
        high = g.astype(BF16)
        low = (g - high.astype(F32)).astype(BF16)
        out = jnp.dot(high, heads[...], preferred_element_type=F32)
        out = out + jnp.dot(low, heads[...], preferred_element_type=F32)
        hidden_grad[at] = out
        set_inner(a1, i, games, jnp.where(pre[1, at] > 0, out, 0.0).astype(BF16))

    steps(top)

    @pl.when(role == 0)
    def _():
        def back(step, i):
            at = pl.ds(step * size, size)
            out = hidden_grad[at] + pair_dot(a1, i, games, turned[...])
            set_inner(a0, i, games, jnp.where(pre[0, at] > 0, out, 0.0).astype(BF16))

        steps(back)

    h, a = hs.at[role], acts.at[role]
    right = [a[1 : SIDE + 1, 2 - q : 2 - q + SIDE].reshape(SIDE * SIDE * games, CH) for q in range(3)]
    right = jnp.concatenate(right, axis=1)
    for half, taps in enumerate(((0, 1), (2,))):
        left = [h[p : p + SIDE, 1 : SIDE + 1].reshape(SIDE * SIDE * games, CH) for p in taps]
        found = lax.dot_general(
            jnp.concatenate(left, axis=1),
            right,
            (((0,), (0,)), ((), ())),
            preferred_element_type=F32,
        )
        for n, p in enumerate(taps):
            for q in range(3):
                at = (3 * p + q) * CH
                grad[at : at + CH, :] = found[n * CH : (n + 1) * CH, q * CH : (q + 1) * CH]
        after_half(half)


def learner_scratch():
    padded = (2, SIDE + 2, SIDE + 2, 16, CH)
    return [
        pltpu.VMEM(padded, BF16),
        pltpu.VMEM(padded, BF16),
        pltpu.VMEM((PACKED, 2 * CH), BF16),
        pltpu.VMEM((2, 1600, CH), F32),
        pltpu.VMEM((1600, CH), F32),
        pltpu.VMEM((SIDE, SIDE, CH), F32),
        pltpu.VMEM((CH, CH), BF16),
        pltpu.VMEM((8, CH), F32),
    ]


def actor_part(given, weights, scratch, games, out, start, ready):
    h0, h1, cells, heads = scratch
    heads[...] = spread_heads(given, games, 4)
    cells[...] = jnp.zeros(cells.shape, F32)
    mine = own_lane(games)
    ready(0)

    def layer_one(step, i):
        _, h = advance(h0, i, games, weights.at[0])
        set_inner(h1, i, games, h)

    steps(layer_one)
    ready(1)

    def layer_two(step, i):
        _, h = advance(h1, i, games, weights.at[1])
        found = head_cells(h, heads, mine, games).reshape(ROWS, SIDE, CH)
        for part in range(ROWS):
            cells[pl.ds((i + part) * SIDE, SIDE), :] = found[part]

    steps(layer_two)
    logits = cells[...]
    cell_id = lax.broadcasted_iota(jnp.int32, logits.shape, 0)
    exps = jnp.where(cell_id < CELLS, jnp.exp(logits), 0.0)
    log_total = jnp.log(lane_sum(jnp.sum(exps, axis=0, keepdims=True), games))
    turned = (logits - log_total).T
    for d in range(4):
        out[pl.ds(start, games), d * CELLS : (d + 1) * CELLS] = turned[
            d * games : (d + 1) * games, 0:CELLS
        ]


def actor_scratch(games):
    padded = (SIDE + 2, SIDE + 2, games, CH)
    return [
        pltpu.VMEM(padded, BF16),
        pltpu.VMEM(padded, BF16),
        pltpu.VMEM((CH, CH), F32),
        pltpu.VMEM((CH, CH), BF16),
    ]


def learner_kernel(traj, given, torso, grad, weights, sem, *scratch):
    hs, acts = scratch[:2]
    for layer in range(2):
        clear_rim(hs.at[layer])
        clear_rim(acts.at[layer])
    copy = pltpu.make_async_copy(traj, center(hs.at[0]), sem)
    copy.start()
    weights[...] = jnp.zeros(weights.shape, BF16)
    pack_layer(weights, torso, 0)
    copy.wait()
    learner_part(given, torso, grad, weights, scratch, lambda half: None)


def learner(traj, given, torso):
    return pl.pallas_call(
        learner_kernel,
        out_shape=jax.ShapeDtypeStruct((TAPS, CH), F32),
        in_specs=[pl.BlockSpec(memory_space=pl.ANY), vmem(), vmem()],
        out_specs=vmem(),
        scratch_shapes=[pltpu.VMEM((2, PACKED, 2 * CH), BF16), pltpu.SemaphoreType.DMA]
        + learner_scratch(),
        compiler_params=pltpu.CompilerParams(vmem_limit_bytes=48 << 20),
    )(traj, given, torso)


def actor_kernel(games, boards, given, torso, out, weights, sem, *scratch):
    h0, h1 = scratch[:2]
    clear_rim(h0)
    clear_rim(h1)
    start = pl.multiple_of(lax.axis_index("role") * games, games)
    copy = pltpu.make_async_copy(boards.at[:, :, pl.ds(start, games)], center(h0), sem)
    copy.start()
    weights[...] = jnp.zeros(weights.shape, BF16)
    for layer in range(2):
        pack_layer(weights, torso, layer)
    copy.wait()
    actor_part(given, weights, scratch, games, out, 0, lambda layer: None)


def actor(boards, given, torso, games):
    return pl.pallas_call(
        functools.partial(actor_kernel, games),
        out_shape=jax.ShapeDtypeStruct((games, 4 * CELLS), F32),
        in_specs=[pl.BlockSpec(memory_space=pl.ANY), vmem(), vmem()],
        out_specs=vmem(),
        scratch_shapes=[pltpu.VMEM((2, PACKED, 2 * CH), BF16), pltpu.SemaphoreType.DMA]
        + actor_scratch(games),
        compiler_params=pltpu.CompilerParams(vmem_limit_bytes=48 << 20),
    )(boards, given, torso)


def step_kernel(games, boards, traj, *refs):
    parts, (torso, moment_one, moment_two, share_out, out), scratch = refs[:7], refs[7:12], refs[12:]
    (weights, full, torso_in, one_in, two_in, grad, plane, quarter, line, norms) = scratch[:10]
    (s1, r1, s2, r2, sn, rn, sz, rz, sp, rp, ss, rs, loads, send_out, recv_out) = scratch[10:25]
    learner_refs, actor_refs = scratch[25:33], scratch[33:37]
    given, part_refs = scratch[37], scratch[38:]
    share = moment_one.shape[0]
    role = lax.axis_index("role")
    dp = lax.axis_index("dp")
    z, spot = dp // 4, dp % 4
    owner = z // 2 == role
    start = pl.multiple_of(role * games, games)

    def send(src, dst, send_sem, recv_sem, to_role, to_dp):
        copy = pltpu.make_async_remote_copy(
            src_ref=src,
            dst_ref=dst,
            send_sem=send_sem,
            recv_sem=recv_sem,
            device_id=(to_role, to_dp),
            device_id_type=MESH,
        )
        return copy

    barrier = pltpu.get_barrier_semaphore()

    def greet(to_role, to_dp):
        pl.semaphore_signal(barrier, inc=1, device_id=(to_role, to_dp), device_id_type=MESH)

    @pl.when(owner)
    def _():
        for k in range(1, 16):
            other = (dp + k) % 16
            greet(other // 8, other)
        for o in range(2):
            greet(role, (2 - 2 * role + o) * 4 + spot)
        greet(1 - role, dp)

    @pl.when(jnp.logical_not(owner))
    def _():
        for k in range(1, 4):
            greet(role, z * 4 + (spot + k) % 4)
            greet(role, ((z + k) % 4) * 4 + spot)
        greet(1 - role, dp)

    hs, acts = learner_refs[:2]
    clear_rim(hs.at[0])
    load_traj = pltpu.make_async_copy(traj, center(hs.at[0]), loads.at[0])
    load_torso = pltpu.make_async_copy(torso, torso_in, loads.at[1])
    load_one = pltpu.make_async_copy(moment_one, one_in, loads.at[2])
    load_two = pltpu.make_async_copy(moment_two, two_in, loads.at[3])
    load_torso.start()
    load_traj.start()
    clear_rim(actor_refs[0])
    load_boards = pltpu.make_async_copy(
        boards.at[:, :, pl.ds(start, games)], center(actor_refs[0]), loads.at[4]
    )
    load_parts = [
        pltpu.make_async_copy(part, ref, loads.at[5 + n])
        for n, (part, ref) in enumerate(zip(parts, part_refs))
    ]
    for load in load_parts:
        load.start()
    load_one.start()
    load_two.start()
    load_boards.start()
    clear_rim(hs.at[1])
    clear_rim(acts.at[0])
    clear_rim(acts.at[1])
    clear_rim(actor_refs[1])
    for load in load_parts:
        load.wait()
    policy_ref, value_ref, length_ref = part_refs[:3]
    given[...] = jnp.zeros(given.shape, F32)
    given[0:4, :] = policy_ref[...].astype(F32)
    given[4:5, :] = value_ref[...].astype(F32)
    given[5:6, :] = jnp.broadcast_to(length_ref[...].astype(F32), (1, CH))
    for n, ref in enumerate(part_refs[3:]):
        given[8 + n : 9 + n, 0:16] = ref[...].astype(F32)
    weights[...] = jnp.zeros(weights.shape, BF16)
    load_torso.wait()
    pack_layer(weights, torso_in, 0)
    load_traj.wait()

    def rows(index):
        return pl.ds(pl.multiple_of(index * share, 8), share)

    def to_plane(o, k):
        p = (spot + k) % 4
        return send(
            grad.at[rows(4 * o + p)],
            plane.at[o, spot],
            s1.at[o, k - 1],
            r1.at[o, spot],
            role,
            z * 4 + p,
        )

    def from_plane(o, k):
        p = (spot + k) % 4
        return send(
            grad.at[rows(4 * o + p)], plane.at[o, p], s1.at[o, k - 1], r1.at[o, p], role, z * 4 + p
        )

    def after_half(half):
        if half == 0:

            @pl.when(owner)
            def _():
                pl.semaphore_wait(barrier, 18)

            @pl.when(jnp.logical_not(owner))
            def _():
                pl.semaphore_wait(barrier, 7)

        for k in range(1, 4):
            to_plane(half, k).start()

    learner_part(given, torso_in, grad, weights, learner_refs, after_half)
    load_one.wait()
    load_two.wait()
    load_boards.wait()

    def to_owner(o):
        return send(
            quarter.at[o], line.at[z], s2.at[o], r2.at[z], role, (2 * role + o) * 4 + spot
        )

    for o in range(2):
        summed = grad[rows(4 * o + spot)]
        for k in range(1, 4):
            from_plane(o, k).wait_recv()
            summed = summed + plane[o, (spot + k) % 4]
        quarter[o] = summed

        @pl.when(z != 2 * role + o)
        def _():
            to_owner(o).start()

    others = tuple((spot + k) % 4 for k in range(1, 4))
    places = (spot,) + others

    def share_of(o, place, to_role=None):
        group = role if to_role is None else to_role
        return full.at[rows((2 * group + o) * 4 + place)]

    def to_near(o, a):
        at = share_of(o, spot)
        return send(at, at, sp.at[o, a], rp.at[o, 2 - a], role, z * 4 + others[a])

    def from_near(o, a):
        at = share_of(o, others[a])
        return send(at, at, sp.at[o, a], rp.at[o, a], role, z * 4 + others[a])

    def to_sibling(o, n):
        at = share_of(o, places[n])
        return send(at, at, ss.at[o, n], rs.at[o, n], 1 - role, dp)

    def to_norm(k):
        other = (dp + k) % 16
        return send(norms.at[dp], norms.at[dp], sn.at[k - 1], rn.at[dp], other // 8, other)

    def from_norm(k):
        other = (dp + k) % 16
        return send(norms.at[other], norms.at[other], sn.at[k - 1], rn.at[other], other // 8, other)

    def down_line(k):
        return send(
            full.at[rows(dp)],
            full.at[rows(dp)],
            sz.at[k - 1],
            rz.at[z % 2],
            role,
            ((z + k) % 4) * 4 + spot,
        )

    @pl.when(owner)
    def _():
        summed = quarter[z % 2]
        for k in range(1, 4):
            other = (z + k) % 4
            send(
                quarter.at[0], line.at[other], s2.at[0], r2.at[other], role, other * 4 + spot
            ).wait_recv()
            summed = summed + line[other]
        norms[dp] = jnp.sum((summed * summed).reshape(share // 8, 8, CH), axis=0)
        for k in range(1, 16):
            to_norm(k).start()
        for k in range(1, 16):
            from_norm(k).wait_recv()
        square_sum = jnp.sum(jnp.sum(norms[...], axis=0), axis=0, keepdims=True)
        square_sum = jnp.sum(square_sum, axis=1, keepdims=True)
        size = float(torso.shape[0] * torso.shape[1])
        factor = jnp.minimum(1.0, jnp.sqrt(jnp.full((1, 1), size, F32)) / jnp.sqrt(square_sum + NORM_EPS))
        clipped = summed * factor
        one = BETA_ONE * one_in[...] + (1.0 - BETA_ONE) * clipped
        two = BETA_TWO * two_in[...] + (1.0 - BETA_TWO) * clipped * clipped
        full[rows(dp)] = torso_in[rows(dp)] - LEARN_RATE * one / (jnp.sqrt(two) + ADAM_EPS)
        for k in range(1, 4):
            down_line(k).start()
        for a in range(3):
            to_near(z % 2, a).start()
        to_sibling(z % 2, 0).start()

    same = 1 - (z // 2 + role - 2 * (z // 2) * role)
    first = same * (z % 2) + (1 - same) * (1 - role)
    for o in (first, 1 - first):

        @pl.when(z != 2 * role + o)
        def _():
            at = share_of(o, spot)
            send(at, at, sz.at[0], rz.at[o], role, (2 * role + o) * 4 + spot).wait_recv()
            for a in range(3):
                to_near(o, a).start()
            to_sibling(o, 0).start()

    for o in (first, 1 - first):
        for a in range(3):
            from_near(o, a).wait_recv()
            to_sibling(o, 1 + a).start()

    for o in range(2):
        for k in range(1, 4):
            to_plane(o, k).wait_send()

        @pl.when(z != 2 * role + o)
        def _():
            to_owner(o).wait_send()

    @pl.when(owner)
    def _():
        for k in range(1, 16):
            to_norm(k).wait_send()
        for k in range(1, 4):
            down_line(k).wait_send()

    def from_sibling():
        for o in range(2):
            for n in range(4):
                at = share_of(o, places[n], 1 - role)
                send(at, at, ss.at[o, n], rs.at[o, n], 1 - role, dp).wait_recv()

    def ready(layer):
        @pl.when(role == 1 - layer)
        def _():
            from_sibling()

        pack_layer(weights, full, layer)

    actor_part(given, weights, actor_refs, games, out, start, ready)
    mine = out.at[pl.ds(start, games)]
    send(mine, mine, send_out, recv_out, 1 - role, dp).start()
    share_out[...] = full[rows(dp)]
    for o in range(2):
        for a in range(3):
            to_near(o, a).wait_send()
        for n in range(4):
            to_sibling(o, n).wait_send()
    theirs = out.at[pl.ds(pl.multiple_of((1 - role) * games, games), games)]
    send(mine, theirs, send_out, recv_out, 1 - role, dp).wait_recv()
    send(mine, mine, send_out, recv_out, 1 - role, dp).wait_send()


def step_call(boards, traj, parts, torso, moment_one, moment_two):
    share, games = moment_one.shape[0], boards.shape[2] // 2
    dma = pltpu.SemaphoreType.DMA
    return pl.pallas_call(
        functools.partial(step_kernel, games),
        out_shape=(
            jax.ShapeDtypeStruct((share, CH), F32),
            jax.ShapeDtypeStruct((2 * games, 4 * CELLS), F32),
        ),
        in_specs=[pl.BlockSpec(memory_space=pl.ANY) for _ in range(12)],
        out_specs=(vmem(), vmem()),
        scratch_shapes=[
            pltpu.VMEM((2, PACKED, 2 * CH), BF16),
            pltpu.VMEM((2 * TAPS, CH), F32),
            pltpu.VMEM((2 * TAPS, CH), F32),
            pltpu.VMEM((share, CH), F32),
            pltpu.VMEM((share, CH), F32),
            pltpu.VMEM((TAPS, CH), F32),
            pltpu.VMEM((2, 4, share, CH), F32),
            pltpu.VMEM((2, share, CH), F32),
            pltpu.VMEM((4, share, CH), F32),
            pltpu.VMEM((16, 8, CH), F32),
            dma((2, 3)),
            dma((2, 4)),
            dma((2,)),
            dma((4,)),
            dma((15,)),
            dma((16,)),
            dma((3,)),
            dma((2,)),
            dma((2, 3)),
            dma((2, 3)),
            dma((2, 4)),
            dma((2, 4)),
            dma((12,)),
            dma,
            dma,
        ]
        + learner_scratch()
        + actor_scratch(games)
        + [pltpu.VMEM((16, CH), F32)]
        + [pltpu.VMEM(part.shape, part.dtype) for part in parts],
        compiler_params=pltpu.CompilerParams(
            collective_id=0, has_side_effects=True, vmem_limit_bytes=56 << 20
        ),
    )(boards, traj, *parts, torso, moment_one, moment_two)


def finish_kernel(share, logp, share_out, logp_out, share_at, logp_at, sems):
    reads = [
        pltpu.make_async_copy(share, share_at, sems.at[0]),
        pltpu.make_async_copy(logp, logp_at, sems.at[1]),
    ]
    writes = [
        pltpu.make_async_copy(share_at, share_out, sems.at[2]),
        pltpu.make_async_copy(logp_at, logp_out, sems.at[3]),
    ]
    for read in reads:
        read.start()
    for read, write in zip(reads, writes):
        read.wait()
        write.start()
    for write in writes:
        write.wait()


def finish(share, logp):
    where = pl.BlockSpec(memory_space=pl.ANY)
    return pl.pallas_call(
        finish_kernel,
        out_shape=(
            jax.ShapeDtypeStruct(share.shape, F32),
            jax.ShapeDtypeStruct(logp.shape, F32),
        ),
        in_specs=[where, where],
        out_specs=(where, where),
        scratch_shapes=[
            pltpu.VMEM(share.shape, F32),
            pltpu.VMEM(logp.shape, F32),
            pltpu.SemaphoreType.DMA((4,)),
        ],
        compiler_params=pltpu.CompilerParams(vmem_limit_bytes=60 << 20),
    )(share, logp)


def update_any(grad, torso, moment_one, moment_two):
    share = moment_one.shape[0]
    summed = lax.all_gather(lax.psum(grad, "dp"), "role", axis=0, tiled=True)
    start = lax.axis_index("dp") * share
    square_sum = jnp.sum(summed * summed)
    factor = jnp.minimum(1.0, jnp.sqrt(float(summed.size)) / jnp.sqrt(square_sum + NORM_EPS))
    clipped = lax.dynamic_slice_in_dim(summed, start, share, 0) * factor
    one = BETA_ONE * moment_one + (1.0 - BETA_ONE) * clipped
    two = BETA_TWO * moment_two + (1.0 - BETA_TWO) * clipped * clipped
    old = lax.dynamic_slice_in_dim(torso, start, share, 0)
    new = old - LEARN_RATE * one / (jnp.sqrt(two) + ADAM_EPS)
    return lax.all_gather(new, "dp", axis=0, tiled=True)


def join_kernel(part, out, send_sem, recv_sem):
    games = part.shape[0]
    role = lax.axis_index("role")
    dp = lax.axis_index("dp")
    barrier = pltpu.get_barrier_semaphore()
    pl.semaphore_signal(barrier, inc=1, device_id=(1 - role, dp), device_id_type=MESH)
    pl.semaphore_wait(barrier, 1)
    mine = pl.ds(pl.multiple_of(role * games, 8), games)
    copy = pltpu.make_async_remote_copy(
        src_ref=part,
        dst_ref=out.at[mine],
        send_sem=send_sem,
        recv_sem=recv_sem,
        device_id=(1 - role, dp),
        device_id_type=MESH,
    )
    copy.start()
    out[mine] = part[...]
    copy.wait()


def join(part):
    return pl.pallas_call(
        join_kernel,
        out_shape=jax.ShapeDtypeStruct((2 * part.shape[0], part.shape[1]), F32),
        in_specs=[vmem()],
        out_specs=vmem(),
        scratch_shapes=[pltpu.SemaphoreType.DMA, pltpu.SemaphoreType.DMA],
        compiler_params=pltpu.CompilerParams(collective_id=1, has_side_effects=True),
    )(part)


def body(
    board_now,
    traj_boards,
    actions,
    lengths,
    behaviour,
    regular,
    rewards,
    torso,
    policy_head,
    value_head,
    first_moment,
    second_moment,
):
    boards = jnp.transpose(board_now, (1, 2, 0, 3))
    traj = jnp.transpose(traj_boards[0], (1, 2, 0, 3))
    if lax.axis_size("dp") == 16 and lax.axis_size("role") == 2:
        parts = (policy_head.T, value_head[None, :], lengths[:, None])
        parts = parts + (actions, behaviour, regular, rewards)
        return finish(*step_call(boards, traj, parts, torso, first_moment, second_moment))

    def wide(x):
        return jnp.pad(x.astype(F32), ((0, 0), (0, CH - x.shape[1])))

    given = jnp.concatenate(
        [
            policy_head.T.astype(F32),
            value_head[None, :].astype(F32),
            jnp.broadcast_to(lengths.astype(F32)[:, None], (1, CH)),
            jnp.zeros((2, CH), F32),
            wide(actions),
            wide(behaviour),
            wide(regular),
            wide(rewards),
            jnp.zeros((4, CH), F32),
        ],
        axis=0,
    )
    grad = learner(traj, given, torso)
    weights = update_any(grad, torso, first_moment, second_moment)
    share_rows = first_moment.shape[0]
    start = lax.axis_index("dp") * share_rows
    new_share = lax.dynamic_slice_in_dim(weights, start, share_rows, 0)
    part = actor(boards, given, weights, board_now.shape[0] // 2)
    return (new_share, join(part))


def solution(mesh):
    return jax.shard_map(
        body,
        mesh=mesh,
        in_specs=(
            P("dp", None, None, None),
            P("dp", None, None, None, None),
            P("dp", None),
            P("dp"),
            P("dp", None),
            P("dp", None),
            P("dp", None),
            P(),
            P(),
            P(),
            P("dp", None),
            P("dp", None),
        ),
        out_specs=(P("dp", None), P("dp", None)),
        check_vma=False,
    )
```
